256 devices in a mesh: row: 16 (over z_lo, y), col: 16 (over x, z_hi, core).
Axes of the slice: x: 4, y: 4, z: 8 (z_hi: 2, z_lo: 4; z = z_hi * 4 + z_lo), core: 2. Of those that a mesh axis runs over, the one named last changes fastest.
Arguments:
- points: bfloat16 [4096, 64], P('row'), may hold values from -1.5 to 1.5
- pivots: int32 [512], replicated, may hold values from 0 to 266239, as said below
- right_values: float32 [4096, 16], P('row'), may hold values from -6 to 6
- right_derivs: float32 [4096, 1024], P('row'), may hold values from -6 to 6
Outputs:
- solution_values: float32 [4096, 16], P(('row', 'col'))
- solution_derivs: float32 [4096, 1024], P(('row', 'col'))
- residual_values: float32 [4096, 16], P(('row', 'col'))
- residual_derivs: float32 [4096, 1024], P(('row', 'col'))
The draws below stay inside these ranges and needn't reach their ends.
Inputs may be any that keep to these rules, and one draw needn't show every extreme that they name: `pivots`: distinct unknown numbers; the first and the last unknown are always among them.
All inputs are finite; a program needn't handle non-finite values.
Results may differ from the reference program's by a relative error of at most 0.0045.
The reference program's roundings to bfloat16 on the way count: a program that leaves them out, or rounds other values in their place, can miss the bound.
Values may be sent and summed in bfloat16 or wider, within the bound.
No kernel may reach another device: no remote copies, remote signals or barrier semaphores. Data moves between devices by JAX's collectives and lax.ppermute only.
A program may use at most 64 MiB of HBM per device.

```python
import math
import jax
import jax.numpy as jnp
from jax import lax

D = 64
RANK = 512
RHS = 16
ITERS = 2
NPTS = 4096


def draw_pivots(key, part):
    unknowns = NPTS * (D + 1)
    first_key = jax.random.fold_in(key, 11)
    second_key = jax.random.fold_in(key, 23)
    inner_ids = jax.random.permutation(first_key, unknowns - 2)[:RANK - 2].astype(jnp.int32) + 1
    joined = jnp.concatenate([jnp.array([0, unknowns - 1], dtype=jnp.int32), inner_ids])
    return jax.random.permutation(second_key, joined).astype(jnp.int32)


def block_levels(key, extent, cuts, low, top_value):
    loudness, own = 1.0, jax.random.fold_in(key, 6)
    for position, parts in cuts:
        draws = jnp.exp(jax.random.uniform(jax.random.fold_in(own, position), (parts,), jnp.float32, low / len(cuts), top_value / len(cuts)))
        loudness = loudness * jnp.repeat(draws, extent[position] // parts).reshape([-1 if axis == position else 1 for axis in range(len(extent))])
    return loudness


def noise(own_key, shape, width, limit, pieces=(), held_as=jnp.bfloat16):
    factor_of = block_levels(own_key, shape, pieces, -0.22, 0.18) if pieces else 1.0
    result = jax.random.normal(own_key, shape, jnp.float32) * width * factor_of
    return jnp.minimum(jnp.maximum(result, -limit), limit).astype(held_as)


def setup_inputs(seed: int = 0) -> dict:
    key_of = jax.random.split(jax.random.key(seed), 5)
    return {
        "points": noise(key_of[0], (NPTS, D), (2.0 * D ** -0.5), 1.5, ((0, 16),)),
        "pivots": draw_pivots(jax.random.fold_in(key_of[4], 71), 0),
        "right_values": noise(key_of[2], (NPTS, RHS), 1.0, 6.0, ((0, 16),), jnp.float32),
        "right_derivs": noise(key_of[3], (NPTS, D * RHS), 1.0, 6.0, ((0, 16),), jnp.float32),
    }


NOISE = 0.5

def contract(former, latter, shared_axis):
    return lax.dot_general(former.astype(jnp.float32), latter.astype(jnp.float32), (((shared_axis,), (shared_axis,)), ((), ())), precision=lax.Precision.HIGHEST, preferred_element_type=jnp.float32)

def float_product(former, latter):
    return jnp.dot(former.astype(jnp.float32), latter.astype(jnp.float32), precision=lax.Precision.HIGHEST, preferred_element_type=jnp.float32)

def kernel_block(former, latter):
    former_norm = jnp.sum(jnp.square(former.astype(jnp.float32)), axis=1)
    latter_norm = jnp.sum(jnp.square(latter.astype(jnp.float32)), axis=1)
    between = contract(former, latter, 1)
    return jnp.exp(-0.5 * (former_norm[:, None] + latter_norm[None, :] - 2.0 * between))

def pivot_table(all_points, pivots):
    features = all_points.shape[1]
    owner_ids = pivots // (features + 1)
    component = pivots % (features + 1)
    pivot_pts = jnp.take(all_points, owner_ids, axis=0)
    valued = (component == 0).astype(jnp.float32)
    unit_dirs = (component[:, None] - 1 == jnp.arange(features, dtype=jnp.int32)[None, :]).astype(jnp.bfloat16)
    chosen = jnp.sum(pivot_pts.astype(jnp.float32) * unit_dirs.astype(jnp.float32), axis=1)
    return (pivot_pts, valued, unit_dirs, chosen)

def factor_rows(own_points, pivot_data):
    pivot_pts, valued, unit_dirs, chosen = pivot_data
    kernel = kernel_block(own_points, pivot_pts)
    along_dirs = contract(own_points, unit_dirs, 1) - chosen[None, :]
    leading = kernel * (valued[None, :] + along_dirs)
    offsets = own_points.astype(jnp.float32)[:, :, None] - jnp.transpose(pivot_pts.astype(jnp.float32))[None, :, :]
    slopes = kernel[:, None, :] * jnp.transpose(unit_dirs.astype(jnp.float32))[None, :, :] - offsets * leading[:, None, :]
    return (leading.astype(jnp.bfloat16), slopes.astype(jnp.bfloat16))

def pivot_block(pivot_data):
    pivot_pts, valued, unit_dirs, chosen = pivot_data
    kernel = kernel_block(pivot_pts, pivot_pts)
    select = contract(pivot_pts, unit_dirs, 1)
    after_terms = select - chosen[None, :]
    before = chosen[:, None] - jnp.transpose(select)
    unit_dots = contract(unit_dirs, unit_dirs, 1)
    mixed_terms = valued[:, None] * valued[None, :] + valued[:, None] * after_terms - valued[None, :] * before
    return kernel * (mixed_terms + unit_dots - before * after_terms)

def solve_inner(chol_factor, target):
    middle = lax.linalg.triangular_solve(chol_factor, target, left_side=True, lower=True)
    return lax.linalg.triangular_solve(chol_factor, middle, left_side=True, lower=True, transpose_a=True)

def per_sample(array_in, samples):
    return jnp.sum(array_in.reshape(array_in.shape[0], -1, samples), axis=(0, 1))

def project(leading, slopes, values_here, derivs_here):
    point_count, features, rank_count = slopes.shape
    samples = values_here.shape[1]
    flat_slopes = slopes.reshape(point_count * features, rank_count)
    half_derivs = derivs_here.astype(jnp.bfloat16).reshape(point_count * features, samples)
    projection = contract(leading, values_here.astype(jnp.bfloat16), 0) + contract(flat_slopes, half_derivs, 0)
    squares = jnp.sum(values_here * values_here, axis=0) + per_sample(derivs_here * derivs_here, samples)
    return (projection, squares)

def descend(chol_factor, projection, leading, slopes, values_here, derivs_here):
    point_count, features, rank_count = slopes.shape
    coefficients = solve_inner(chol_factor, projection)
    flat_slopes = slopes.reshape(point_count * features, rank_count)
    new_values = (values_here - float_product(leading, coefficients)) / NOISE
    new_derivs = (derivs_here - float_product(flat_slopes, coefficients).reshape(point_count, -1)) / NOISE
    return (coefficients, new_values, new_derivs)

def apply_inverse(points, pivot_data, chol_factor, values_all, derivs_all, block_rows):
    samples = values_all.shape[1]
    rank_count = chol_factor.shape[0]
    pts_blocks = points.reshape((-1, block_rows) + points.shape[1:])
    val_blocks = values_all.reshape(-1, block_rows, samples)
    der_blocks = derivs_all.reshape(-1, block_rows, derivs_all.shape[1])

    def gather_step(running, pack_items):
        pts_here, values_here, derivs_here = pack_items
        leading, slopes = factor_rows(pts_here, pivot_data)
        proj_here, unused = project(leading, slopes, values_here, derivs_here)
        return (running + proj_here, None)
    projection, unused = lax.scan(gather_step, jnp.zeros((rank_count, samples), jnp.float32), (pts_blocks, val_blocks, der_blocks))

    def descend_step(pack_items):
        pts_here, values_here, derivs_here = pack_items
        leading, slopes = factor_rows(pts_here, pivot_data)
        return descend(chol_factor, projection, leading, slopes, values_here, derivs_here)
    unused_coef, new_values, new_derivs = lax.map(descend_step, (pts_blocks, val_blocks, der_blocks))
    return (new_values.reshape(values_all.shape), new_derivs.reshape(derivs_all.shape))

def operator_image(points, kmat, search_values, search_derivs):
    point_count, features = points.shape
    samples = search_values.shape[1]
    base_terms = float_product(kmat, search_derivs)
    points_wide = points.astype(jnp.float32)
    sample_derivs = jnp.transpose(search_derivs.reshape(point_count, features, samples), (2, 0, 1))

    def one_sample(pack_items):
        head_vals, slopes_here = pack_items
        owned_dots = jnp.sum(points_wide * slopes_here, axis=1)
        cross_terms = float_product(points, jnp.transpose(slopes_here))
        weight = kmat * (head_vals[None, :] + cross_terms - owned_dots[None, :])
        summed = jnp.sum(weight, axis=1)
        moved_sum = float_product(weight, points)
        return (summed, moved_sum)
    summed, moved_sum = lax.map(one_sample, (jnp.transpose(search_values), sample_derivs))
    image_values = jnp.transpose(summed)
    extra_terms = jnp.transpose(moved_sum, (1, 2, 0)).reshape(point_count, features * samples)
    image_derivs = base_terms - (points_wide[:, :, None] * image_values[:, None, :]).reshape(point_count, -1) + extra_terms
    return (image_values + NOISE * search_values, image_derivs + NOISE * search_derivs)

def reference(points, pivots, right_values, right_derivs):
    point_count, features = points.shape
    samples = right_values.shape[1]
    block_rows = math.gcd(point_count, 512)
    pivot_data = pivot_table(points, pivots)
    rank_count = pivots.shape[0]

    def gram_step(running, pts_here):
        leading, slopes = factor_rows(pts_here, pivot_data)
        flat_slopes = slopes.reshape(-1, rank_count)
        return (running + contract(leading, leading, 0) + contract(flat_slopes, flat_slopes, 0), None)
    gram, unused = lax.scan(gram_step, jnp.zeros((rank_count, rank_count), jnp.float32), points.reshape((-1, block_rows) + points.shape[1:]))
    chol_factor = jnp.linalg.cholesky(NOISE * pivot_block(pivot_data) + gram)
    kmat = kernel_block(points, points)

    def inner(values_a, derivs_a, values_b, derivs_b):
        return jnp.sum(values_a * values_b, axis=0) + per_sample(derivs_a * derivs_b, samples)
    estimate_values = jnp.zeros_like(right_values)
    estimate_derivs = jnp.zeros_like(right_derivs)
    remain_values, remain_derivs = (right_values, right_derivs)
    search_values, search_derivs = apply_inverse(points, pivot_data, chol_factor, remain_values, remain_derivs, block_rows)
    gamma_now = inner(remain_values, remain_derivs, search_values, search_derivs)
    for iteration in range(ITERS):
        image_values, image_derivs = operator_image(points, kmat, search_values, search_derivs)
        step_size = gamma_now / inner(search_values, search_derivs, image_values, image_derivs)
        tiled_step = jnp.tile(step_size, features)
        estimate_values = estimate_values + step_size * search_values
        estimate_derivs = estimate_derivs + tiled_step * search_derivs
        remain_values = remain_values - step_size * image_values
        remain_derivs = remain_derivs - tiled_step * image_derivs
        if iteration + 1 < ITERS:
            precond_values, precond_derivs = apply_inverse(points, pivot_data, chol_factor, remain_values, remain_derivs, block_rows)
            gamma_next = inner(remain_values, remain_derivs, precond_values, precond_derivs)
            beta_ratio = gamma_next / gamma_now
            search_values = precond_values + beta_ratio * search_values
            search_derivs = precond_derivs + jnp.tile(beta_ratio, features) * search_derivs
            gamma_now = gamma_next
    return (estimate_values, estimate_derivs, remain_values, remain_derivs)
```

```python
import jax
import jax.numpy as jnp
from jax import lax
from jax.sharding import PartitionSpec as P

ITERS = 2
NOISE = 0.5
HIGHEST = lax.Precision.HIGHEST


def spread(block, axis):
    copies = jnp.broadcast_to(block[None], (lax.axis_size(axis),) + block.shape)
    return lax.all_to_all(copies, axis, 0, 0, tiled=True)


def wide_dot(former, latter, dims):
    return lax.dot_general(
        former.astype(jnp.float32),
        latter.astype(jnp.float32),
        ((dims[0:1], dims[1:2]), ((), ())),
        precision=HIGHEST,
        preferred_element_type=jnp.float32,
    )


def half_dot(former, latter, dims):
    return lax.dot_general(
        former,
        latter,
        ((dims[0:1], dims[1:2]), ((), ())),
        preferred_element_type=jnp.float32,
    )


def pivot_table(all_points, pivots):
    count, features = all_points.shape
    owner_ids = pivots // (features + 1)
    component = pivots % (features + 1)
    picks = (owner_ids[:, None] == jnp.arange(count, dtype=jnp.int32)[None, :]).astype(jnp.bfloat16)
    pivot_pts = half_dot(picks, all_points, (1, 0)).astype(jnp.bfloat16)
    valued = (component == 0).astype(jnp.float32)
    unit_dirs = (component[:, None] - 1 == jnp.arange(features, dtype=jnp.int32)[None, :]).astype(
        jnp.bfloat16
    )
    chosen = jnp.sum(pivot_pts.astype(jnp.float32) * unit_dirs.astype(jnp.float32), axis=1)
    return (pivot_pts, valued, unit_dirs, chosen)


def square_norms(points):
    return jnp.sum(jnp.square(points.astype(jnp.float32)), axis=1)


def factor_rows(own_points, pivot_data):
    pivot_pts, valued, unit_dirs, chosen = pivot_data
    norms = square_norms(own_points)
    dots = half_dot(own_points, pivot_pts, (1, 1))
    kern = jnp.exp(-0.5 * (norms[:, None] + square_norms(pivot_pts)[None, :] - 2.0 * dots))
    along = half_dot(own_points, unit_dirs, (1, 1)) - chosen[None, :]
    lead = kern * (valued[None, :] + along)
    offsets = (
        jnp.transpose(own_points.astype(jnp.float32))[:, :, None]
        - jnp.transpose(pivot_pts.astype(jnp.float32))[:, None, :]
    )
    slopes = (
        kern[None] * jnp.transpose(unit_dirs.astype(jnp.float32))[:, None, :] - offsets * lead[None]
    )
    return jnp.concatenate([lead[None], slopes], axis=0).astype(jnp.bfloat16)


def pivot_block(pivot_data):
    pivot_pts, valued, unit_dirs, chosen = pivot_data
    norms = square_norms(pivot_pts)
    dots = half_dot(pivot_pts, pivot_pts, (1, 1))
    kernel = jnp.exp(-0.5 * (norms[:, None] + norms[None, :] - 2.0 * dots))
    select = half_dot(pivot_pts, unit_dirs, (1, 1))
    after_terms = select - chosen[None, :]
    before = chosen[:, None] - jnp.transpose(select)
    unit_dots = half_dot(unit_dirs, unit_dirs, (1, 1))
    mixed_terms = (
        valued[:, None] * valued[None, :] + valued[:, None] * after_terms - valued[None, :] * before
    )
    return kernel * (mixed_terms + unit_dots - before * after_terms)


def thirds(wide):
    high = lax.reduce_precision(wide, 8, 7)
    middle = lax.reduce_precision(wide - high, 8, 7)
    low = wide - high - middle
    return jnp.stack([high, middle, low]).astype(jnp.bfloat16)


def project(flat_factor, field):
    parts = half_dot(thirds(field.reshape(-1)), flat_factor, (1, 0))
    return jnp.stack([parts[0], parts[0] + (parts[1] + parts[2])])


def expand(flat_factor, coef):
    parts = half_dot(thirds(coef), flat_factor, (1, 1))
    return parts[0] + (parts[1] + parts[2])


def operate(row_points, kmat, points, field, row_field):
    values, derivs = field[:, 0], field[:, 1:]
    owned = values - jnp.sum(points.astype(jnp.float32) * derivs, axis=1)
    weight = kmat * (wide_dot(row_points, derivs, (1, 1)) + owned[None, :])
    moved = wide_dot(weight, points, (1, 0))
    summed = jnp.sum(weight, axis=1, keepdims=True)
    base = wide_dot(kmat, derivs, (1, 0))
    return (
        jnp.concatenate([summed, base - row_points.astype(jnp.float32) * summed + moved], axis=1)
        + NOISE * row_field
    )


def local(points, pivots, right_values, right_derivs):
    row, col = lax.axis_index("row"), lax.axis_index("col")
    row_count, col_count = lax.axis_size("row"), lax.axis_size("col")
    row_total, features = points.shape
    samples = right_values.shape[1]
    rank = pivots.shape[0]
    width = features + 1

    def assemble(blocks):
        return jnp.transpose(blocks, (0, 2, 1)).reshape(row_count * row_total, width)

    all_points = spread(points, "row").reshape(-1, features)
    lanes = jnp.arange(samples * features, dtype=jnp.int32)
    picks = (lanes[None, :] == jnp.arange(features, dtype=jnp.int32)[:, None] * samples + col)
    value_picks = (jnp.arange(samples, dtype=jnp.int32) == col)[None, :]
    residual = jnp.concatenate(
        [wide_dot(value_picks, right_values, (1, 1)), wide_dot(picks, right_derivs, (1, 1))],
        axis=0,
    )

    pivot_data = pivot_table(all_points, pivots)
    factor = factor_rows(points, pivot_data).reshape(width * row_total, rank)
    share = rank // col_count
    block = lax.dynamic_slice_in_dim(factor, col * share, share, 1)
    gram_part = half_dot(block, factor, (0, 0))
    sums = spread(jnp.concatenate([gram_part, project(factor, residual)], axis=0), "row")
    sums = jnp.sum(sums, axis=0)
    gram = spread(sums[:share], "col").reshape(rank, rank)
    chol = jnp.linalg.cholesky(NOISE * pivot_block(pivot_data) + gram)

    def solve(target):
        middle = lax.linalg.triangular_solve(chol, target[:, None], left_side=True, lower=True)
        return lax.linalg.triangular_solve(
            chol, middle, left_side=True, lower=True, transpose_a=True
        )[:, 0]

    kmat = jnp.exp(
        -0.5
        * (
            square_norms(points)[:, None]
            + square_norms(all_points)[None, :]
            - 2.0 * half_dot(points, all_points, (1, 1))
        )
    )

    def total(part):
        return jnp.sum(spread(part[None], "row"), axis=(0, 1))

    def descend(projections, squares, field):
        coef = solve(projections[0])
        descent = (field - expand(factor, coef).reshape(width, row_total)) / NOISE
        return ((squares - jnp.sum(projections[1] * coef)) / NOISE, descent)

    def image_of(direction):
        whole = assemble(spread(direction, "row"))
        own = jnp.transpose(direction)
        return jnp.transpose(operate(points, kmat, all_points, whole, own))

    squares = total(jnp.broadcast_to(jnp.sum(residual * residual), (128,)))[0]
    gamma, direction = descend(sums[share:], squares, residual)
    estimate = jnp.zeros_like(residual)
    for iteration in range(ITERS):
        image = image_of(direction)
        curve = total(jnp.broadcast_to(jnp.sum(direction * image), (128,)))[0]
        step = gamma / curve
        estimate = estimate + step * direction
        residual = residual - step * image
        if iteration + 1 < ITERS:
            part = jnp.concatenate(
                [
                    project(factor, residual).reshape(-1),
                    jnp.broadcast_to(jnp.sum(residual * residual), (128,)),
                ]
            )
            sums = total(part)
            gamma_next, descent = descend(sums[: 2 * rank].reshape(2, rank), sums[-1], residual)
            direction = descent + (gamma_next / gamma) * direction
            gamma = gamma_next
    share_rows = row_total // col_count
    fields = jnp.stack([estimate, residual]).reshape(2, width, col_count, share_rows)
    fields = jnp.transpose(fields, (2, 0, 1, 3)).reshape(col_count, -1)
    fields = lax.all_to_all(fields, "col", 0, 0, tiled=True)
    fields = jnp.transpose(fields.reshape(samples, 2, width, share_rows), (1, 3, 2, 0))
    values, derivs = fields[:, :, 0], fields[:, :, 1:].reshape(2, share_rows, features * samples)
    return (values[0], derivs[0], values[1], derivs[1])


def solution(mesh):
    in_specs = (P("row", None), P(), P("row", None), P("row", None))
    out_specs = (P(("row", "col"), None),) * 4
    return jax.shard_map(local, mesh=mesh, in_specs=in_specs, out_specs=out_specs, check_vma=False)
```

```python
import math

import jax
import jax.numpy as jnp
from jax import lax
from jax.experimental import pallas as pl
from jax.experimental.pallas import tpu as pltpu
from jax.sharding import PartitionSpec as P

ITERS = 2
NOISE = 0.5
HIGHEST = lax.Precision.HIGHEST


def spread(block, axis, groups=None):
    size = len(groups[0]) if groups else lax.axis_size(axis)
    copies = jnp.broadcast_to(block[None], (size,) + block.shape)
    return lax.all_to_all(copies, axis, 0, 0, axis_index_groups=groups, tiled=True)


def wide_dot(former, latter, dims):
    return lax.dot_general(
        former.astype(jnp.float32),
        latter.astype(jnp.float32),
        ((dims[0:1], dims[1:2]), ((), ())),
        precision=HIGHEST,
        preferred_element_type=jnp.float32,
    )


def half_dot(former, latter, dims):
    return lax.dot_general(
        former,
        latter,
        ((dims[0:1], dims[1:2]), ((), ())),
        preferred_element_type=jnp.float32,
    )


def pivot_table(all_points, pivots):
    count, features = all_points.shape
    owner_ids = pivots // (features + 1)
    component = pivots % (features + 1)
    picks = (owner_ids[:, None] == jnp.arange(count, dtype=jnp.int32)[None, :]).astype(jnp.bfloat16)
    pivot_pts = half_dot(picks, all_points, (1, 0)).astype(jnp.bfloat16)
    valued = (component == 0).astype(jnp.float32)
    unit_dirs = (component[:, None] - 1 == jnp.arange(features, dtype=jnp.int32)[None, :]).astype(
        jnp.bfloat16
    )
    chosen = jnp.sum(pivot_pts.astype(jnp.float32) * unit_dirs.astype(jnp.float32), axis=1)
    return (pivot_pts, valued, unit_dirs, chosen, component[:, None] - 1)


def turned(array, start):
    return lax.dynamic_slice_in_dim(jnp.concatenate([array, array]), start, array.shape[0], 0)


def square_norms(points):
    return jnp.sum(jnp.square(points.astype(jnp.float32)), axis=1)


def pivot_block(pivot_data):
    pivot_pts, valued, unit_dirs, chosen, _ = pivot_data
    norms = square_norms(pivot_pts)
    dots = half_dot(pivot_pts, pivot_pts, (1, 1))
    kernel = jnp.exp(-0.5 * (norms[:, None] + norms[None, :] - 2.0 * dots))
    select = half_dot(pivot_pts, unit_dirs, (1, 1))
    after_terms = select - chosen[None, :]
    before = chosen[:, None] - jnp.transpose(select)
    unit_dots = half_dot(unit_dirs, unit_dirs, (1, 1))
    mixed_terms = (
        valued[:, None] * valued[None, :] + valued[:, None] * after_terms - valued[None, :] * before
    )
    return kernel * (mixed_terms + unit_dots - before * after_terms)


def pair_inverse(first, cross, second):
    scale = 1.0 / (first * second - cross * cross)
    return (second * scale, -cross * scale, first * scale)


def sweep_four(mat, j, lane, sub):
    n = mat.shape[0]
    cols = [jnp.broadcast_to(mat[:, j + q : j + q + 1], mat.shape) for q in range(4)]
    top = (j // 8) * 8

    def entry(p, q):
        return jnp.broadcast_to(cols[q][j + p : j + p + 1, :], (8, n))

    p0, p1, p2 = pair_inverse(entry(0, 0), entry(1, 0), entry(1, 1))
    q00, q01, q10, q11 = entry(2, 0), entry(3, 0), entry(2, 1), entry(3, 1)
    t00, t01 = q00 * p0 + q10 * p1, q00 * p1 + q10 * p2
    t10, t11 = q01 * p0 + q11 * p1, q01 * p1 + q11 * p2
    w00 = entry(2, 2) - (t00 * q00 + t01 * q10)
    w01 = entry(3, 2) - (t10 * q00 + t11 * q10)
    w11 = entry(3, 3) - (t10 * q01 + t11 * q11)
    v0, v1, v2 = pair_inverse(w00, w01, w11)
    s00, s01 = v0 * t00 + v1 * t10, v0 * t01 + v1 * t11
    s10, s11 = v1 * t00 + v2 * t10, v1 * t01 + v2 * t11
    i00 = p0 + (t00 * s00 + t10 * s10)
    i01 = p1 + (t00 * s01 + t10 * s11)
    i11 = p2 + (t01 * s01 + t11 * s11)
    inv = (
        (i00, i01, -s00, -s10),
        (i01, i11, -s01, -s11),
        (-s00, -s01, v0, v1),
        (-s10, -s11, v1, v2),
    )
    inside = (lane >= j) & (lane < j + 4)
    rows = [
        jnp.where(
            inside,
            jnp.where(lane == j + q, 1.0, 0.0),
            jnp.broadcast_to(mat[j + q : j + q + 1, :], (8, n)),
        )
        for q in range(4)
    ]
    pivot_rows = [
        (inv[p][0] * rows[0] + inv[p][1] * rows[1]) + (inv[p][2] * rows[2] + inv[p][3] * rows[3])
        for p in range(4)
    ]
    tiles = []
    for s in range(0, n, 8):
        tile = jnp.where(inside, 0.0, mat[s : s + 8])
        terms = [cols[p][s : s + 8] * pivot_rows[p] for p in range(4)]
        tile = tile - ((terms[0] + terms[1]) + (terms[2] + terms[3]))
        if s == top:
            for p in range(4):
                tile = jnp.where(sub == j - top + p, pivot_rows[p], tile)
        tiles.append(tile)
    return jnp.concatenate(tiles, axis=0)


SWEEP = 128
VMEM = pl.BlockSpec(memory_space=pltpu.VMEM)
SHARE = 32


def inverse_kernel(turn_ref, bands_ref, kpp_ref, out_ref, diag_ref):
    size = out_ref.shape[0]
    bands = size // SHARE
    lane = lax.broadcasted_iota(jnp.int32, (SHARE, 128), 1)
    for k in range(bands):
        packed = bands_ref[k, 2 * SHARE : 2 * SHARE + 8]
        corner = jnp.concatenate(
            [packed] + [pltpu.roll(packed, 128 - SHARE * u, 1) for u in range(1, 4)], axis=0
        )
        band = jnp.concatenate(
            [
                jnp.where(lane < SHARE, 0.5, 1.0) * bands_ref[k, 0:SHARE],
                bands_ref[k, SHARE : 2 * SHARE],
                jnp.where(lane < SHARE, 0.5 * corner, 0.0),
                jnp.zeros((SHARE, size - 384), jnp.float32),
            ],
            axis=1,
        )
        place = pl.multiple_of(lax.rem(k + bands - turn_ref[0], bands) * SHARE, SHARE)
        out_ref[pl.ds(place, SHARE)] = pltpu.roll(band, place, 1)
    out_ref[...] = out_ref[...] + jnp.transpose(out_ref[...]) + NOISE * kpp_ref[...]
    lane = lax.broadcasted_iota(jnp.int32, (8, SWEEP), 1)
    sub = lax.broadcasted_iota(jnp.int32, (8, SWEEP), 0)
    identity = jnp.where(
        lax.broadcasted_iota(jnp.int32, (SWEEP, SWEEP), 0)
        == lax.broadcasted_iota(jnp.int32, (SWEEP, SWEEP), 1),
        1.0,
        0.0,
    )

    def block_step(k, carry):
        here = pl.ds(pl.multiple_of(k * SWEEP, SWEEP), SWEEP)
        diag = out_ref[here, here]
        for j in range(0, SWEEP, 4):
            diag = sweep_four(diag, j, lane, sub)
        diag_ref[...] = diag
        column = out_ref[:, here]
        out_ref[here, here] = identity
        row = jnp.dot(
            diag_ref[...], out_ref[here, :], precision=HIGHEST, preferred_element_type=jnp.float32
        )
        out_ref[:, here] = jnp.zeros((size, SWEEP), jnp.float32)
        out_ref[...] = out_ref[...] - jnp.dot(
            column, row, precision=HIGHEST, preferred_element_type=jnp.float32
        )
        out_ref[here, :] = row
        return carry

    lax.fori_loop(0, size // SWEEP, block_step, 0)


def inverse(turn, bands, kpp):
    vmem = pl.BlockSpec(memory_space=pltpu.VMEM)
    return pl.pallas_call(
        inverse_kernel,
        out_shape=jax.ShapeDtypeStruct(kpp.shape, jnp.float32),
        in_specs=[pl.BlockSpec(memory_space=pltpu.SMEM), vmem, vmem],
        out_specs=vmem,
        scratch_shapes=[pltpu.VMEM((SWEEP, SWEEP), jnp.float32)],
        compiler_params=pltpu.CompilerParams(vmem_limit_bytes=20 * 2**20),
        cost_estimate=pl.CostEstimate(
            flops=10**9, bytes_accessed=3 * 2**20, transcendentals=0
        ),
    )(turn, bands, kpp)


def dot_nt(former, latter):
    return lax.dot_general(
        former, latter, (((1,), (1,)), ((), ())), preferred_element_type=jnp.float32
    )


def thirds_rows(row, count):
    high = row.astype(jnp.bfloat16).astype(jnp.float32)
    middle = (row - high).astype(jnp.bfloat16).astype(jnp.float32)
    low = row - high - middle
    sub = lax.broadcasted_iota(jnp.int32, (count, row.shape[1]), 0)
    parts = jnp.where(
        sub == 0, high, jnp.where(sub == 1, middle, jnp.where(sub == 2, low, jnp.zeros_like(low)))
    )
    return parts.astype(jnp.bfloat16)


def plain_rows(m, u, columns, turned_ref, lead):
    return (columns[:, u : u + 1] - turned_ref[pl.ds(m, 1)]) * lead


def each_dimension(pivots_ref, columns_ref, features, start, body):
    columns_ref[:, 0:features] = pivots_ref[...].astype(jnp.float32)

    def group(step, carry):
        columns = columns_ref[...]
        for u in range(UNROLL):
            carry = body(step * UNROLL + u, u, columns, carry)
        columns_ref[...] = pltpu.roll(columns, columns.shape[1] - UNROLL, 1)
        return carry

    return lax.fori_loop(0, features // UNROLL, group, start)


def factor_kernel(
    pivots_ref, dirs_ref, comp_ref, points_ref, turned_ref, field_ref,
    lead_ref, extra_ref, sums_ref, kern_ref, comps_ref, total_ref, columns_ref,
):
    features = turned_ref.shape[0]
    rank = lead_ref.shape[0]

    def add(rows, line):
        left = jnp.concatenate([rows[:SHARE], thirds_rows(line, 16)], axis=0)
        total_ref[...] += dot_nt(left, rows)

    pivot_pts = pivots_ref[...]
    wide_pts = pivot_pts.astype(jnp.float32)
    wide_dirs = dirs_ref[...].astype(jnp.float32)
    norms = jnp.sum(wide_pts * wide_pts, axis=1, keepdims=True)
    chosen = jnp.sum(wide_pts * wide_dirs, axis=1, keepdims=True)
    valued = jnp.where(comp_ref[...] < 0, 1.0, 0.0)
    own_norms = jnp.sum(turned_ref[...] * turned_ref[...], axis=0, keepdims=True)
    dots = dot_nt(pivot_pts, points_ref[...])
    kern = jnp.exp(-0.5 * (own_norms + norms - 2.0 * dots))
    along = dot_nt(dirs_ref[...], points_ref[...]) - chosen
    lead = kern * (valued + along)
    kern_ref[...] = kern
    lead_ref[...] = lead
    plain = -along * lead
    extra = (kern + plain).astype(jnp.bfloat16).astype(jnp.float32) - plain.astype(
        jnp.bfloat16
    ).astype(jnp.float32)
    extra_ref[...] = jnp.where(comp_ref[...] < 0, 0.0, extra)
    comps_ref[...] = jnp.broadcast_to(comp_ref[...], comps_ref.shape)
    total_ref[...] = jnp.zeros_like(total_ref)
    add(lead.astype(jnp.bfloat16), field_ref[features : features + 1])

    def body(m, u, columns, carry):
        plain = plain_rows(m, u, columns, turned_ref, lead_ref[...])
        rows = jnp.where(comps_ref[...] == m, kern_ref[...] + plain, plain)
        add(rows.astype(jnp.bfloat16), field_ref[pl.ds(m, 1)])
        return carry

    each_dimension(pivots_ref, columns_ref, features, 0, body)
    sums_ref[0:SHARE] = total_ref[0:SHARE, 0:128]
    sums_ref[SHARE : 2 * SHARE] = total_ref[0:SHARE, 128:256]
    lane = lax.broadcasted_iota(jnp.int32, (8, 128), 1)
    corner = jnp.zeros((8, 128), jnp.float32)
    for u in range(4):
        piece = total_ref[8 * u : 8 * u + 8, 256:384]
        piece = pltpu.roll(piece, SHARE * u, 1) if u else piece
        corner = jnp.where((lane >= SHARE * u) & (lane < SHARE * (u + 1)), piece, corner)
    sums_ref[2 * SHARE : 2 * SHARE + 8] = corner
    high = total_ref[SHARE : SHARE + 1]
    full = high + (total_ref[SHARE + 1 : SHARE + 2] + total_ref[SHARE + 2 : SHARE + 3])
    for u in range(rank // 128):
        sums_ref[72 + u : 73 + u] = high[:, 128 * u : 128 * u + 128]
        sums_ref[76 + u : 77 + u] = full[:, 128 * u : 128 * u + 128]
    field = field_ref[0 : features + 1]
    square = jnp.sum(jnp.sum(field * field, axis=0, keepdims=True), axis=1, keepdims=True)
    sums_ref[80:88] = jnp.broadcast_to(square, (8, 128))


UNROLL = 8


def make_factor(pivot_data, points, turned_points, field):
    pivot_pts, comp, dirs = pivot_data
    rank, features = pivot_pts.shape
    count = points.shape[0]
    return pl.pallas_call(
        factor_kernel,
        in_specs=[VMEM] * 6,
        out_specs=[VMEM] * 3,
        out_shape=[
            jax.ShapeDtypeStruct((rank, count), jnp.float32),
            jax.ShapeDtypeStruct((rank, count), jnp.float32),
            jax.ShapeDtypeStruct((88, 128), jnp.float32),
        ],
        scratch_shapes=[
            pltpu.VMEM((rank, count), jnp.float32),
            pltpu.VMEM((rank, count), jnp.int32),
            pltpu.VMEM((SHARE + 16, rank), jnp.float32),
            pltpu.VMEM((rank, 128), jnp.float32),
        ],
        compiler_params=pltpu.CompilerParams(vmem_limit_bytes=20 * 2**20),
        cost_estimate=pl.CostEstimate(
            flops=2 * 48 * 65 * rank * count, bytes_accessed=4 * 2**20, transcendentals=rank * count
        ),
    )(pivot_pts, dirs, comp, points, turned_points, field)


def descend_kernel(
    pivots_ref, turned_ref, lead_ref, extra_ref, picks_ref, inv_ref, sums_ref, field_ref, old_ref,
    gamma_ref, out_ref, new_gamma_ref, coef_ref, columns_ref,
):
    features = field_ref.shape[0] - 1
    lines = sums_ref[...]
    low = jnp.concatenate([lines[u : u + 1] for u in range(4)], axis=1)
    full = jnp.concatenate([lines[u : u + 1] for u in range(4, 8)], axis=1)
    coef = jnp.dot(
        jnp.broadcast_to(low, (8, low.shape[1])),
        inv_ref[...],
        precision=HIGHEST,
        preferred_element_type=jnp.float32,
    )[0:1]
    coef_ref[...] = thirds_rows(coef, 16)
    gamma = (lines[8:9, 0:1] - jnp.sum(full * coef, axis=1, keepdims=True)) / NOISE
    new_gamma_ref[...] = jnp.broadcast_to(gamma, (8, 128))
    beta = gamma / gamma_ref[0:1, 0:1]

    def apply(rows):
        parts = jnp.dot(
            coef_ref[...], rows.astype(jnp.bfloat16), preferred_element_type=jnp.float32
        )
        return parts[0:1] + (parts[1:2] + parts[2:3])

    out_ref[features : features + 1] = apply(lead_ref[...])
    out_ref[0:features] = jnp.dot(
        picks_ref[...].astype(jnp.float32) * coef,
        extra_ref[...],
        precision=HIGHEST,
        preferred_element_type=jnp.float32,
    )

    def body(m, u, columns, carry):
        out_ref[pl.ds(m, 1)] += apply(plain_rows(m, u, columns, turned_ref, lead_ref[...]))
        return carry

    each_dimension(pivots_ref, columns_ref, features, 0, body)
    out_ref[...] = (field_ref[...] - out_ref[...]) / NOISE + beta * old_ref[...]


def descend(factor, inv, sums, field, old, gamma):
    rank, count = factor[2].shape
    return pl.pallas_call(
        descend_kernel,
        in_specs=[VMEM] * 10,
        out_specs=[VMEM] * 2,
        out_shape=[
            jax.ShapeDtypeStruct(field.shape, jnp.float32),
            jax.ShapeDtypeStruct((8, 128), jnp.float32),
        ],
        scratch_shapes=[pltpu.VMEM((16, rank), jnp.bfloat16), pltpu.VMEM((rank, 128), jnp.float32)],
        compiler_params=pltpu.CompilerParams(vmem_limit_bytes=20 * 2**20),
        cost_estimate=pl.CostEstimate(
            flops=2 * 16 * 65 * rank * count, bytes_accessed=5 * 2**20, transcendentals=0
        ),
    )(*factor, inv, sums, field, old, gamma)


def project_kernel(
    pivots_ref, turned_ref, lead_ref, extra_ref, picks_ref, image_ref, field_ref, curve_ref,
    gamma_ref, next_ref, sums_ref, step_ref, columns_ref,
):
    features = field_ref.shape[0] - 1
    curve = curve_ref[0, 0:1, 0:1]
    for k in range(1, curve_ref.shape[0]):
        curve = curve + curve_ref[k, 0:1, 0:1]
    scale = gamma_ref[0:1, 0:1] / curve
    step_ref[...] = jnp.broadcast_to(scale, (8, 128))
    next_ref[...] = field_ref[...] - scale * image_ref[...]

    def add(line, rows):
        return dot_nt(thirds_rows(line, 16), rows.astype(jnp.bfloat16))

    total = add(next_ref[features : features + 1], lead_ref[...])

    def body(m, u, columns, total):
        rows = plain_rows(m, u, columns, turned_ref, lead_ref[...])
        return total + add(next_ref[pl.ds(m, 1)], rows)

    total = each_dimension(pivots_ref, columns_ref, features, total, body)
    field = next_ref[...]
    upper = field[0:features].astype(jnp.bfloat16)
    rest = field[0:features] - upper.astype(jnp.float32)
    middle = rest.astype(jnp.bfloat16)
    lower = (rest - middle.astype(jnp.float32)).astype(jnp.bfloat16)

    def meet(part):
        return lax.dot_general(
            picks_ref[...], part, (((0,), (0,)), ((), ())), preferred_element_type=jnp.float32
        )

    first = meet(upper)
    ones = jnp.ones((8, field.shape[1]), jnp.float32)
    both = [
        lax.dot_general(
            ones,
            extra_ref[...] * part,
            (((1,), (1,)), ((), ())),
            precision=HIGHEST,
            preferred_element_type=jnp.float32,
        )[0:1]
        for part in (first, first + (meet(middle) + meet(lower)))
    ]
    high = total[0:1] + both[0]
    full = total[0:1] + (total[1:2] + total[2:3]) + both[1]
    for u in range(high.shape[1] // 128):
        sums_ref[u : 1 + u] = high[:, 128 * u : 128 * u + 128]
        sums_ref[4 + u : 5 + u] = full[:, 128 * u : 128 * u + 128]
    square = jnp.sum(jnp.sum(field * field, axis=0, keepdims=True), axis=1, keepdims=True)
    sums_ref[8:16] = jnp.broadcast_to(square, (8, 128))


def project(factor, image, field, curve, gamma):
    rank, count = factor[2].shape
    return pl.pallas_call(
        project_kernel,
        in_specs=[VMEM] * 9,
        out_specs=[VMEM] * 3,
        out_shape=[
            jax.ShapeDtypeStruct(field.shape, jnp.float32),
            jax.ShapeDtypeStruct((16, 128), jnp.float32),
            jax.ShapeDtypeStruct((8, 128), jnp.float32),
        ],
        scratch_shapes=[pltpu.VMEM((rank, 128), jnp.float32)],
        compiler_params=pltpu.CompilerParams(vmem_limit_bytes=20 * 2**20),
        cost_estimate=pl.CostEstimate(
            flops=2 * 16 * 65 * rank * count, bytes_accessed=4 * 2**20, transcendentals=0
        ),
    )(*factor, image, field, curve, gamma)


def image_kernel(fields_ref, row_points_ref, col_points_ref, image_ref):
    blocks, width, count = fields_ref.shape
    features = width - 1

    def dot(former, latter):
        return jnp.dot(former, latter, preferred_element_type=jnp.float32)

    sides = []
    for k in range(blocks):
        points = col_points_ref[k]
        spare = jnp.zeros((count, features), jnp.float32)
        wide = jnp.concatenate([points.astype(jnp.float32), spare], axis=1)
        turned_points = jnp.transpose(wide)[0:features]
        lane = lax.broadcasted_iota(jnp.int32, wide.shape, 1)
        with_ones = jnp.where(lane == features, 1.0, wide).astype(jnp.bfloat16)
        slopes = fields_ref[k, 0:features]
        owned = fields_ref[k, features : features + 1] - jnp.sum(
            turned_points * slopes, axis=0, keepdims=True
        )
        norms = jnp.sum(turned_points * turned_points, axis=0, keepdims=True)
        high = slopes.astype(jnp.bfloat16)
        rest = slopes - high.astype(jnp.float32)
        middle = rest.astype(jnp.bfloat16)
        low = (rest - middle.astype(jnp.float32)).astype(jnp.bfloat16)
        sides.append((with_ones, owned, norms, high, middle, low))

    def rows(j, carry):
        points = row_points_ref[j]
        wide = points.astype(jnp.float32)
        own_norms = jnp.sum(wide * wide, axis=1, keepdims=True)
        thrice = jnp.concatenate([points] * 3, axis=1)
        total = jnp.zeros((count, 2 * features), jnp.float32)
        base = jnp.zeros((count, 2 * features), jnp.float32)
        for k in range(blocks):
            with_ones, owned, norms, high, middle, low = sides[k]
            dots = dot_nt(points, col_points_ref[k])
            kern = jnp.exp(-0.5 * (own_norms + norms - 2.0 * dots))
            cross = dot(thrice, jnp.concatenate([high, middle, low], axis=0))
            weight = kern * (cross + owned)
            upper = weight.astype(jnp.bfloat16)
            lower = (weight - upper.astype(jnp.float32)).astype(jnp.bfloat16)
            total += dot(upper, with_ones) + dot(lower, with_ones)
            upper = kern.astype(jnp.bfloat16)
            lower = (kern - upper.astype(jnp.float32)).astype(jnp.bfloat16)
            base += dot_nt(upper, jnp.concatenate([high, middle], axis=0)) + dot_nt(
                lower, jnp.concatenate([high, jnp.zeros_like(high)], axis=0)
            )
        value = total[:, features : features + 1]
        spare = jnp.zeros((count, features), jnp.float32)
        total += jnp.concatenate(
            [base[:, 0:features] + base[:, features:] - wide * value, spare], axis=1
        )
        image_ref[j] = jnp.transpose(total)[0:width]
        return carry

    lax.fori_loop(0, row_points_ref.shape[0], rows, 0)


def image_part(fields, row_points, col_points):
    blocks, width, count = fields.shape
    return pl.pallas_call(
        image_kernel,
        in_specs=[VMEM] * 3,
        out_specs=VMEM,
        out_shape=jax.ShapeDtypeStruct((row_points.shape[0], width, count), jnp.float32),
        compiler_params=pltpu.CompilerParams(vmem_limit_bytes=24 * 2**20),
        cost_estimate=pl.CostEstimate(
            flops=2 * 5 * blocks * blocks * count * count * 128,
            bytes_accessed=2**20,
            transcendentals=blocks * blocks * count * count,
        ),
    )(fields, row_points, col_points)


def gather_kernel(parts_ref, own_ref, image_ref, curve_ref):
    image = NOISE * own_ref[...]
    for k in range(parts_ref.shape[0]):
        image = image + parts_ref[k]
    image_ref[...] = image
    curve = jnp.sum(own_ref[...] * image, axis=0, keepdims=True)
    curve_ref[...] = jnp.broadcast_to(
        jnp.sum(curve, axis=1, keepdims=True)[None], curve_ref.shape
    )


def gather_image(parts, own, devices):
    return pl.pallas_call(
        gather_kernel,
        in_specs=[VMEM] * 2,
        out_specs=[VMEM] * 2,
        out_shape=[
            jax.ShapeDtypeStruct(own.shape, jnp.float32),
            jax.ShapeDtypeStruct((devices, 8, 128), jnp.float32),
        ],
    )(parts, own)


def advance_kernel(curve_ref, gamma_ref, sides_ref, moves_ref, out_ref):
    curve = curve_ref[0, 0:1, 0:1]
    for k in range(1, curve_ref.shape[0]):
        curve = curve + curve_ref[k, 0:1, 0:1]
    scale = gamma_ref[0:1, 0:1] / curve
    out_ref[0] = sides_ref[0] + scale * moves_ref[0]
    out_ref[1] = sides_ref[1] - scale * moves_ref[1]


def local(points, pivots, right_values, right_derivs):
    row, col = lax.axis_index("row"), lax.axis_index("col")
    row_count, col_count = lax.axis_size("row"), lax.axis_size("col")
    row_total, features = points.shape
    samples = right_values.shape[1]
    width = features + 1

    side = math.isqrt(row_count)
    by_high = [[high * side + low for high in range(side)] for low in range(side)]
    by_low = [[high * side + low for low in range(side)] for high in range(side)]
    point_blocks = spread(points, "row")
    grid_blocks = point_blocks.reshape((side, side) + points.shape)
    row_points = lax.dynamic_index_in_dim(grid_blocks, row // side, 0, keepdims=False)
    col_points = lax.dynamic_index_in_dim(grid_blocks, row % side, 1, keepdims=False)
    all_points = point_blocks.reshape(-1, features)
    lanes = jnp.arange(samples * features, dtype=jnp.int32)
    picks = (lanes[None, :] == jnp.arange(features, dtype=jnp.int32)[:, None] * samples + col)
    value_picks = (jnp.arange(samples, dtype=jnp.int32) == col)[None, :]
    residual = jnp.concatenate(
        [wide_dot(picks, right_derivs, (1, 1)), wide_dot(value_picks, right_values, (1, 1))],
        axis=0,
    )

    pivot_data = pivot_table(all_points, turned(pivots, col * SHARE))
    own_turned = jnp.transpose(points.astype(jnp.float32))
    rank = pivots.shape[0]
    lead, extra, sums = make_factor(
        (pivot_data[0], pivot_data[4], pivot_data[2]), points, own_turned, residual
    )
    factor = (pivot_data[0], own_turned, lead, extra, jnp.transpose(pivot_data[2]))
    sums = jnp.sum(spread(jnp.sum(spread(sums, "row", by_high), axis=0), "row", by_low), axis=0)
    inv = inverse(col[None], spread(sums[:72], "col"), pivot_block(pivot_data))

    gamma = jnp.ones((8, 128), jnp.float32)
    direction, gamma = descend(
        factor, inv, sums[72:], residual, jnp.zeros_like(residual), gamma
    )
    estimate = jnp.zeros_like(residual)
    for iteration in range(ITERS):
        fields = spread(direction, "row", by_high)
        parts = lax.all_to_all(
            image_part(fields, row_points, col_points),
            "row", 0, 0, axis_index_groups=by_low, tiled=True,
        )
        image, curve = gather_image(parts, direction, row_count)
        curve = lax.all_to_all(curve, "row", 0, 0, tiled=True)
        if iteration + 1 < ITERS:
            residual, sums, step = project(factor, image, residual, curve, gamma)
            estimate = step[0, 0] * direction
            sums = jnp.sum(spread(sums, "row"), axis=0)
            direction, gamma = descend(factor, inv, sums, residual, direction, gamma)
    fields = pl.pallas_call(
        advance_kernel,
        in_specs=[VMEM] * 4,
        out_specs=VMEM,
        out_shape=jax.ShapeDtypeStruct((2, width, row_total), jnp.float32),
    )(curve, gamma, jnp.stack([estimate, residual]), jnp.stack([direction, image]))
    share_rows = row_total // col_count
    fields = fields.reshape(2, width, col_count, share_rows)
    fields = jnp.transpose(fields, (2, 0, 1, 3)).reshape(col_count, -1)
    fields = lax.all_to_all(fields, "col", 0, 0, tiled=True)
    fields = jnp.transpose(fields.reshape(samples, 2, width, share_rows), (1, 3, 2, 0))
    values = fields[:, :, features]
    derivs = fields[:, :, :features].reshape(2, share_rows, features * samples)
    return (values[0], derivs[0], values[1], derivs[1])


def solution(mesh):
    in_specs = (P("row", None), P(), P("row", None), P("row", None))
    out_specs = (P(("row", "col"), None),) * 4
    return jax.shard_map(local, mesh=mesh, in_specs=in_specs, out_specs=out_specs, check_vma=False)
```

```python
import math

import jax
import jax.numpy as jnp
from jax import lax
from jax.experimental import pallas as pl
from jax.experimental.pallas import tpu as pltpu
from jax.sharding import PartitionSpec as P

ITERS = 2
NOISE = 0.5
HIGHEST = lax.Precision.HIGHEST


def spread(block, axis, groups=None):
    size = len(groups[0]) if groups else lax.axis_size(axis)
    copies = jnp.broadcast_to(block[None], (size,) + block.shape)
    return lax.all_to_all(copies, axis, 0, 0, axis_index_groups=groups, tiled=True)


def wide_dot(former, latter, dims):
    return lax.dot_general(
        former.astype(jnp.float32),
        latter.astype(jnp.float32),
        ((dims[0:1], dims[1:2]), ((), ())),
        precision=HIGHEST,
        preferred_element_type=jnp.float32,
    )


def half_dot(former, latter, dims):
    return lax.dot_general(
        former,
        latter,
        ((dims[0:1], dims[1:2]), ((), ())),
        preferred_element_type=jnp.float32,
    )


def pivot_table(all_points, pivots):
    count, features = all_points.shape
    owner_ids = pivots // (features + 1)
    component = pivots % (features + 1)
    picks = (owner_ids[:, None] == jnp.arange(count, dtype=jnp.int32)[None, :]).astype(jnp.bfloat16)
    pivot_pts = half_dot(picks, all_points, (1, 0)).astype(jnp.bfloat16)
    valued = (component == 0).astype(jnp.float32)
    unit_dirs = (component[:, None] - 1 == jnp.arange(features, dtype=jnp.int32)[None, :]).astype(
        jnp.bfloat16
    )
    chosen = jnp.sum(pivot_pts.astype(jnp.float32) * unit_dirs.astype(jnp.float32), axis=1)
    return (pivot_pts, valued, unit_dirs, chosen, component[:, None] - 1)


def turned(array, start):
    return lax.dynamic_slice_in_dim(jnp.concatenate([array, array]), start, array.shape[0], 0)


def square_norms(points):
    return jnp.sum(jnp.square(points.astype(jnp.float32)), axis=1)


def pivot_block(pivot_data):
    pivot_pts, valued, unit_dirs, chosen, _ = pivot_data
    norms = square_norms(pivot_pts)
    dots = half_dot(pivot_pts, pivot_pts, (1, 1))
    kernel = jnp.exp(-0.5 * (norms[:, None] + norms[None, :] - 2.0 * dots))
    select = half_dot(pivot_pts, unit_dirs, (1, 1))
    after_terms = select - chosen[None, :]
    before = chosen[:, None] - jnp.transpose(select)
    unit_dots = half_dot(unit_dirs, unit_dirs, (1, 1))
    mixed_terms = (
        valued[:, None] * valued[None, :] + valued[:, None] * after_terms - valued[None, :] * before
    )
    return kernel * (mixed_terms + unit_dots - before * after_terms)


def pair_inverse(first, cross, second):
    scale = 1.0 / (first * second - cross * cross)
    return (second * scale, -cross * scale, first * scale)


def inverse_four(a):
    p0, p1, p2 = pair_inverse(a(0, 0), a(1, 0), a(1, 1))
    q00, q01, q10, q11 = a(2, 0), a(3, 0), a(2, 1), a(3, 1)
    t00, t01 = q00 * p0 + q10 * p1, q00 * p1 + q10 * p2
    t10, t11 = q01 * p0 + q11 * p1, q01 * p1 + q11 * p2
    w00 = a(2, 2) - (t00 * q00 + t01 * q10)
    w01 = a(3, 2) - (t10 * q00 + t11 * q10)
    w11 = a(3, 3) - (t10 * q01 + t11 * q11)
    v0, v1, v2 = pair_inverse(w00, w01, w11)
    s00, s01 = v0 * t00 + v1 * t10, v0 * t01 + v1 * t11
    s10, s11 = v1 * t00 + v2 * t10, v1 * t01 + v2 * t11
    i00 = p0 + (t00 * s00 + t10 * s10)
    i01 = p1 + (t00 * s01 + t10 * s11)
    i11 = p2 + (t01 * s01 + t11 * s11)
    return (
        (i00, i01, -s00, -s10),
        (i01, i11, -s01, -s11),
        (-s00, -s01, v0, v1),
        (-s10, -s11, v1, v2),
    )


def dot_four(left, right):
    return (left[0] * right[0] + left[1] * right[1]) + (left[2] * right[2] + left[3] * right[3])


def sweep_eight(mat, top, lane, sub):
    n = mat.shape[0]
    cols = [jnp.broadcast_to(mat[:, top + q : top + q + 1], mat.shape) for q in range(8)]

    def entry(p, q):
        p, q = max(p, q), min(p, q)
        return jnp.broadcast_to(cols[q][top + p : top + p + 1, :], (8, n))

    cross = [[entry(4 + q, k) for q in range(4)] for k in range(4)]
    first = inverse_four(entry)
    turn = [[dot_four(first[k], [cross[l][q] for l in range(4)]) for q in range(4)] for k in range(4)]

    def left_over(p, q):
        return entry(4 + p, 4 + q) - dot_four(
            [cross[k][p] for k in range(4)], [turn[k][q] for k in range(4)]
        )

    second = inverse_four(left_over)
    front = (lane >= top) & (lane < top + 4)
    back = (lane >= top + 4) & (lane < top + 8)
    inside = front | back
    unit = [jnp.where(lane == top + p, 1.0, 0.0) for p in range(8)]
    rows = [jnp.broadcast_to(mat[top + p : top + p + 1, :], (8, n)) for p in range(8)]
    ahead = [jnp.where(front, unit[p], rows[p]) for p in range(4)]
    ahead = [dot_four(first[k], ahead) for k in range(4)]
    after = [
        jnp.where(
            back,
            unit[4 + p],
            jnp.where(front, 0.0, rows[4 + p]) - dot_four([cross[k][p] for k in range(4)], ahead),
        )
        for p in range(4)
    ]
    after = [dot_four(second[p], after) for p in range(4)]
    ahead = [jnp.where(back, 0.0, ahead[k]) - dot_four(turn[k], after) for k in range(4)]
    pivot_rows = ahead + after
    tiles = []
    for s in range(0, n, 8):
        if s == top:
            tile = pivot_rows[0]
            for p in range(1, 8):
                tile = jnp.where(sub == p, pivot_rows[p], tile)
        else:
            here = [cols[p][s : s + 8] for p in range(8)]
            tile = jnp.where(inside, 0.0, mat[s : s + 8]) - (
                dot_four(here[:4], pivot_rows[:4]) + dot_four(here[4:], pivot_rows[4:])
            )
        tiles.append(tile)
    return jnp.concatenate(tiles, axis=0)


SWEEP = 128
VMEM = pl.BlockSpec(memory_space=pltpu.VMEM)
SHARE = 32


def inverse_kernel(turn_ref, bands_ref, kpp_ref, out_ref, diag_ref):
    size = out_ref.shape[0]
    bands = size // SHARE
    lane = lax.broadcasted_iota(jnp.int32, (SHARE, 128), 1)
    for k in range(bands):
        packed = bands_ref[k, 2 * SHARE : 2 * SHARE + 8]
        corner = jnp.concatenate(
            [packed] + [pltpu.roll(packed, 128 - SHARE * u, 1) for u in range(1, 4)], axis=0
        )
        band = jnp.concatenate(
            [
                jnp.where(lane < SHARE, 0.5, 1.0) * bands_ref[k, 0:SHARE],
                bands_ref[k, SHARE : 2 * SHARE],
                jnp.where(lane < SHARE, 0.5 * corner, 0.0),
                jnp.zeros((SHARE, size - 384), jnp.float32),
            ],
            axis=1,
        )
        place = pl.multiple_of(lax.rem(k + bands - turn_ref[0], bands) * SHARE, SHARE)
        out_ref[pl.ds(place, SHARE)] = pltpu.roll(band, place, 1)
    out_ref[...] = out_ref[...] + jnp.transpose(out_ref[...]) + NOISE * kpp_ref[...]
    lane = lax.broadcasted_iota(jnp.int32, (8, SWEEP), 1)
    sub = lax.broadcasted_iota(jnp.int32, (8, SWEEP), 0)

    def dot(former, latter):
        return jnp.dot(former, latter, precision=HIGHEST, preferred_element_type=jnp.float32)

    count = size // SWEEP
    spans = [slice(k * SWEEP, (k + 1) * SWEEP) for k in range(count)]
    diag = out_ref[spans[0], spans[0]]
    for k in range(count):
        for top in range(0, SWEEP, 8):
            diag = sweep_eight(diag, top, lane, sub)
        diag_ref[...] = diag
        here = diag_ref[...]
        row = [here if c == k else dot(here, out_ref[spans[k], spans[c]]) for c in range(count)]
        if k + 1 < count:
            ahead = spans[k + 1]
            diag = out_ref[ahead, ahead] - dot(out_ref[ahead, spans[k]], row[k + 1])
        for r in range(count):
            if r == k:
                continue
            column = out_ref[spans[r], spans[k]]
            for c in range(count):
                if c == k:
                    out_ref[spans[r], spans[c]] = -dot(column, here)
                elif r == c == k + 1:
                    out_ref[spans[r], spans[c]] = diag
                else:
                    out_ref[spans[r], spans[c]] = out_ref[spans[r], spans[c]] - dot(column, row[c])
        for c in range(count):
            out_ref[spans[k], spans[c]] = row[c]


def inverse(turn, bands, kpp):
    vmem = pl.BlockSpec(memory_space=pltpu.VMEM)
    return pl.pallas_call(
        inverse_kernel,
        out_shape=jax.ShapeDtypeStruct(kpp.shape, jnp.float32),
        in_specs=[pl.BlockSpec(memory_space=pltpu.SMEM), vmem, vmem],
        out_specs=vmem,
        scratch_shapes=[pltpu.VMEM((SWEEP, SWEEP), jnp.float32)],
        compiler_params=pltpu.CompilerParams(vmem_limit_bytes=20 * 2**20),
        cost_estimate=pl.CostEstimate(
            flops=10**9, bytes_accessed=3 * 2**20, transcendentals=0
        ),
    )(turn, bands, kpp)


def dot_nt(former, latter):
    return lax.dot_general(
        former, latter, (((1,), (1,)), ((), ())), preferred_element_type=jnp.float32
    )


def thirds_rows(row, count):
    high = row.astype(jnp.bfloat16).astype(jnp.float32)
    middle = (row - high).astype(jnp.bfloat16).astype(jnp.float32)
    low = row - high - middle
    sub = lax.broadcasted_iota(jnp.int32, (count, row.shape[1]), 0)
    parts = jnp.where(
        sub == 0, high, jnp.where(sub == 1, middle, jnp.where(sub == 2, low, jnp.zeros_like(low)))
    )
    return parts.astype(jnp.bfloat16)


def plain_rows(m, u, columns, turned_ref, lead):
    return (columns[:, u : u + 1] - turned_ref[pl.ds(m, 1)]) * lead


def each_dimension(pivots_ref, columns_ref, features, start, body):
    columns_ref[:, 0:features] = pivots_ref[...].astype(jnp.float32)

    def group(step, carry):
        columns = columns_ref[...]
        for u in range(UNROLL):
            carry = body(step * UNROLL + u, u, columns, carry)
        columns_ref[...] = pltpu.roll(columns, columns.shape[1] - UNROLL, 1)
        return carry

    return lax.fori_loop(0, features // UNROLL, group, start)


def factor_kernel(
    pivots_ref, dirs_ref, comp_ref, points_ref, turned_ref, field_ref,
    lead_ref, extra_ref, sums_ref, kern_ref, comps_ref, total_ref, columns_ref,
):
    features = turned_ref.shape[0]
    rank = lead_ref.shape[0]

    def add(rows, line):
        left = jnp.concatenate([rows[:SHARE], thirds_rows(line, 16)], axis=0)
        total_ref[...] += dot_nt(left, rows)

    pivot_pts = pivots_ref[...]
    wide_pts = pivot_pts.astype(jnp.float32)
    wide_dirs = dirs_ref[...].astype(jnp.float32)
    norms = jnp.sum(wide_pts * wide_pts, axis=1, keepdims=True)
    chosen = jnp.sum(wide_pts * wide_dirs, axis=1, keepdims=True)
    valued = jnp.where(comp_ref[...] < 0, 1.0, 0.0)
    own_norms = jnp.sum(turned_ref[...] * turned_ref[...], axis=0, keepdims=True)
    dots = dot_nt(pivot_pts, points_ref[...])
    kern = jnp.exp(-0.5 * (own_norms + norms - 2.0 * dots))
    along = dot_nt(dirs_ref[...], points_ref[...]) - chosen
    lead = kern * (valued + along)
    kern_ref[...] = kern
    lead_ref[...] = lead
    plain = -along * lead
    extra = (kern + plain).astype(jnp.bfloat16).astype(jnp.float32) - plain.astype(
        jnp.bfloat16
    ).astype(jnp.float32)
    extra_ref[...] = jnp.where(comp_ref[...] < 0, 0.0, extra)
    comps_ref[...] = jnp.broadcast_to(comp_ref[...], comps_ref.shape)
    total_ref[...] = jnp.zeros_like(total_ref)
    add(lead.astype(jnp.bfloat16), field_ref[features : features + 1])

    def body(m, u, columns, carry):
        plain = plain_rows(m, u, columns, turned_ref, lead_ref[...])
        rows = jnp.where(comps_ref[...] == m, kern_ref[...] + plain, plain)
        add(rows.astype(jnp.bfloat16), field_ref[pl.ds(m, 1)])
        return carry

    each_dimension(pivots_ref, columns_ref, features, 0, body)
    sums_ref[0:SHARE] = total_ref[0:SHARE, 0:128]
    sums_ref[SHARE : 2 * SHARE] = total_ref[0:SHARE, 128:256]
    lane = lax.broadcasted_iota(jnp.int32, (8, 128), 1)
    corner = jnp.zeros((8, 128), jnp.float32)
    for u in range(4):
        piece = total_ref[8 * u : 8 * u + 8, 256:384]
        piece = pltpu.roll(piece, SHARE * u, 1) if u else piece
        corner = jnp.where((lane >= SHARE * u) & (lane < SHARE * (u + 1)), piece, corner)
    sums_ref[2 * SHARE : 2 * SHARE + 8] = corner
    high = total_ref[SHARE : SHARE + 1]
    full = high + (total_ref[SHARE + 1 : SHARE + 2] + total_ref[SHARE + 2 : SHARE + 3])
    for u in range(rank // 128):
        sums_ref[72 + u : 73 + u] = high[:, 128 * u : 128 * u + 128]
        sums_ref[76 + u : 77 + u] = full[:, 128 * u : 128 * u + 128]
    field = field_ref[0 : features + 1]
    square = jnp.sum(jnp.sum(field * field, axis=0, keepdims=True), axis=1, keepdims=True)
    sums_ref[80:88] = jnp.broadcast_to(square, (8, 128))


UNROLL = 8


def make_factor(pivot_data, points, turned_points, field):
    pivot_pts, comp, dirs = pivot_data
    rank, features = pivot_pts.shape
    count = points.shape[0]
    return pl.pallas_call(
        factor_kernel,
        in_specs=[VMEM] * 6,
        out_specs=[VMEM] * 3,
        out_shape=[
            jax.ShapeDtypeStruct((rank, count), jnp.float32),
            jax.ShapeDtypeStruct((rank, count), jnp.float32),
            jax.ShapeDtypeStruct((88, 128), jnp.float32),
        ],
        scratch_shapes=[
            pltpu.VMEM((rank, count), jnp.float32),
            pltpu.VMEM((rank, count), jnp.int32),
            pltpu.VMEM((SHARE + 16, rank), jnp.float32),
            pltpu.VMEM((rank, 128), jnp.float32),
        ],
        compiler_params=pltpu.CompilerParams(vmem_limit_bytes=20 * 2**20),
        cost_estimate=pl.CostEstimate(
            flops=2 * 48 * 65 * rank * count, bytes_accessed=4 * 2**20, transcendentals=rank * count
        ),
    )(pivot_pts, dirs, comp, points, turned_points, field)


def descend_kernel(
    pivots_ref, turned_ref, lead_ref, extra_ref, picks_ref, inv_ref, sums_ref, field_ref, old_ref,
    gamma_ref, out_ref, copies_ref, new_gamma_ref, coef_ref, columns_ref,
):
    features = field_ref.shape[0] - 1
    lines = sums_ref[0]
    for k in range(1, sums_ref.shape[0]):
        lines = lines + sums_ref[k]
    low = jnp.concatenate([lines[u : u + 1] for u in range(4)], axis=1)
    full = jnp.concatenate([lines[u : u + 1] for u in range(4, 8)], axis=1)
    coef = jnp.dot(
        jnp.broadcast_to(low, (8, low.shape[1])),
        inv_ref[...],
        precision=HIGHEST,
        preferred_element_type=jnp.float32,
    )[0:1]
    coef_ref[...] = thirds_rows(coef, 16)
    gamma = (lines[8:9, 0:1] - jnp.sum(full * coef, axis=1, keepdims=True)) / NOISE
    new_gamma_ref[...] = jnp.broadcast_to(gamma, (8, 128))
    beta = gamma / gamma_ref[0:1, 0:1]

    def apply(rows):
        parts = jnp.dot(
            coef_ref[...], rows.astype(jnp.bfloat16), preferred_element_type=jnp.float32
        )
        return parts[0:1] + (parts[1:2] + parts[2:3])

    out_ref[features : features + 1] = apply(lead_ref[...])
    out_ref[0:features] = jnp.dot(
        picks_ref[...].astype(jnp.float32) * coef,
        extra_ref[...],
        precision=HIGHEST,
        preferred_element_type=jnp.float32,
    )

    def body(m, u, columns, carry):
        out_ref[pl.ds(m, 1)] += apply(plain_rows(m, u, columns, turned_ref, lead_ref[...]))
        return carry

    each_dimension(pivots_ref, columns_ref, features, 0, body)
    out_ref[...] = (field_ref[...] - out_ref[...]) / NOISE + beta * old_ref[...]
    copies_ref[...] = jnp.broadcast_to(out_ref[...][None], copies_ref.shape)


def descend(factor, inv, sums, field, old, gamma, copies):
    rank, count = factor[2].shape
    return pl.pallas_call(
        descend_kernel,
        in_specs=[VMEM] * 10,
        out_specs=[VMEM] * 3,
        out_shape=[
            jax.ShapeDtypeStruct(field.shape, jnp.float32),
            jax.ShapeDtypeStruct((copies,) + field.shape, jnp.float32),
            jax.ShapeDtypeStruct((8, 128), jnp.float32),
        ],
        scratch_shapes=[pltpu.VMEM((16, rank), jnp.bfloat16), pltpu.VMEM((rank, 128), jnp.float32)],
        compiler_params=pltpu.CompilerParams(vmem_limit_bytes=20 * 2**20),
        cost_estimate=pl.CostEstimate(
            flops=2 * 16 * 65 * rank * count, bytes_accessed=5 * 2**20, transcendentals=0
        ),
    )(*factor, inv, sums, field, old, gamma)


def project_kernel(
    pivots_ref, turned_ref, lead_ref, extra_ref, picks_ref, image_ref, field_ref, curve_ref,
    gamma_ref, next_ref, sums_ref, step_ref, columns_ref,
):
    features = field_ref.shape[0] - 1
    curve = curve_ref[0, 0:1, 0:1]
    for k in range(1, curve_ref.shape[0]):
        curve = curve + curve_ref[k, 0:1, 0:1]
    scale = gamma_ref[0:1, 0:1] / curve
    step_ref[...] = jnp.broadcast_to(scale, (8, 128))
    next_ref[...] = field_ref[...] - scale * image_ref[...]

    def add(line, rows):
        return dot_nt(thirds_rows(line, 16), rows.astype(jnp.bfloat16))

    total = add(next_ref[features : features + 1], lead_ref[...])

    def body(m, u, columns, total):
        rows = plain_rows(m, u, columns, turned_ref, lead_ref[...])
        return total + add(next_ref[pl.ds(m, 1)], rows)

    total = each_dimension(pivots_ref, columns_ref, features, total, body)
    field = next_ref[...]
    upper = field[0:features].astype(jnp.bfloat16)
    rest = field[0:features] - upper.astype(jnp.float32)
    middle = rest.astype(jnp.bfloat16)
    lower = (rest - middle.astype(jnp.float32)).astype(jnp.bfloat16)

    def meet(part):
        return lax.dot_general(
            picks_ref[...], part, (((0,), (0,)), ((), ())), preferred_element_type=jnp.float32
        )

    first = meet(upper)
    ones = jnp.ones((8, field.shape[1]), jnp.float32)
    both = [
        lax.dot_general(
            ones,
            extra_ref[...] * part,
            (((1,), (1,)), ((), ())),
            precision=HIGHEST,
            preferred_element_type=jnp.float32,
        )[0:1]
        for part in (first, first + (meet(middle) + meet(lower)))
    ]
    high = total[0:1] + both[0]
    full = total[0:1] + (total[1:2] + total[2:3]) + both[1]
    lines = [line[:, 128 * u : 128 * u + 128] for line in (high, full) for u in range(4)]
    square = jnp.sum(jnp.sum(field * field, axis=0, keepdims=True), axis=1, keepdims=True)
    lines = jnp.concatenate(lines + [jnp.broadcast_to(square, (8, 128))], axis=0)
    sums_ref[...] = jnp.broadcast_to(lines[None], sums_ref.shape)


def project(factor, image, field, curve, gamma):
    rank, count = factor[2].shape
    return pl.pallas_call(
        project_kernel,
        in_specs=[VMEM] * 9,
        out_specs=[VMEM] * 3,
        out_shape=[
            jax.ShapeDtypeStruct(field.shape, jnp.float32),
            jax.ShapeDtypeStruct((curve.shape[0], 16, 128), jnp.float32),
            jax.ShapeDtypeStruct((8, 128), jnp.float32),
        ],
        scratch_shapes=[pltpu.VMEM((rank, 128), jnp.float32)],
        compiler_params=pltpu.CompilerParams(vmem_limit_bytes=20 * 2**20),
        cost_estimate=pl.CostEstimate(
            flops=2 * 16 * 65 * rank * count, bytes_accessed=4 * 2**20, transcendentals=0
        ),
    )(*factor, image, field, curve, gamma)


def image_kernel(place_ref, fields_ref, points_ref, image_ref):
    blocks, width, count = fields_ref.shape
    features = width - 1
    high_place, low_place = place_ref[0] // blocks, lax.rem(place_ref[0], blocks)

    def dot(former, latter):
        return jnp.dot(former, latter, preferred_element_type=jnp.float32)

    sides = []
    for k in range(blocks):
        points = points_ref[k * blocks + low_place]
        spare = jnp.zeros((count, features), jnp.float32)
        wide = jnp.concatenate([points.astype(jnp.float32), spare], axis=1)
        turned_points = jnp.transpose(wide)[0:features]
        lane = lax.broadcasted_iota(jnp.int32, wide.shape, 1)
        with_ones = jnp.where(lane == features, 1.0, wide).astype(jnp.bfloat16)
        slopes = fields_ref[k, 0:features]
        owned = fields_ref[k, features : features + 1] - jnp.sum(
            turned_points * slopes, axis=0, keepdims=True
        )
        norms = jnp.sum(turned_points * turned_points, axis=0, keepdims=True)
        high = slopes.astype(jnp.bfloat16)
        rest = slopes - high.astype(jnp.float32)
        middle = rest.astype(jnp.bfloat16)
        low = (rest - middle.astype(jnp.float32)).astype(jnp.bfloat16)
        sides.append((with_ones, owned, norms, high, middle, low))

    def rows(j, carry):
        points = points_ref[high_place * blocks + j]
        wide = points.astype(jnp.float32)
        own_norms = jnp.sum(wide * wide, axis=1, keepdims=True)
        thrice = jnp.concatenate([points] * 3, axis=1)
        total = jnp.zeros((count, 2 * features), jnp.float32)
        base = jnp.zeros((count, 2 * features), jnp.float32)
        for k in range(blocks):
            with_ones, owned, norms, high, middle, low = sides[k]
            dots = dot_nt(points, points_ref[k * blocks + low_place])
            kern = jnp.exp(-0.5 * (own_norms + norms - 2.0 * dots))
            cross = dot(thrice, jnp.concatenate([high, middle, low], axis=0))
            weight = kern * (cross + owned)
            upper = weight.astype(jnp.bfloat16)
            lower = (weight - upper.astype(jnp.float32)).astype(jnp.bfloat16)
            total += dot(upper, with_ones) + dot(lower, with_ones)
            upper = kern.astype(jnp.bfloat16)
            lower = (kern - upper.astype(jnp.float32)).astype(jnp.bfloat16)
            base += dot_nt(upper, jnp.concatenate([high, middle], axis=0)) + dot_nt(
                lower, jnp.concatenate([high, jnp.zeros_like(high)], axis=0)
            )
        value = total[:, features : features + 1]
        spare = jnp.zeros((count, features), jnp.float32)
        total += jnp.concatenate(
            [base[:, 0:features] + base[:, features:] - wide * value, spare], axis=1
        )
        image_ref[j] = jnp.transpose(total)[0:width]
        return carry

    lax.fori_loop(0, blocks, rows, 0)


def image_part(place, fields, points):
    blocks, width, count = fields.shape
    return pl.pallas_call(
        image_kernel,
        in_specs=[pl.BlockSpec(memory_space=pltpu.SMEM), VMEM, VMEM],
        out_specs=VMEM,
        out_shape=jax.ShapeDtypeStruct((blocks, width, count), jnp.float32),
        compiler_params=pltpu.CompilerParams(vmem_limit_bytes=24 * 2**20),
        cost_estimate=pl.CostEstimate(
            flops=2 * 5 * blocks * blocks * count * count * 128,
            bytes_accessed=2**20,
            transcendentals=blocks * blocks * count * count,
        ),
    )(place, fields, points)


def gather_kernel(parts_ref, own_ref, image_ref, curve_ref):
    image = NOISE * own_ref[...]
    for k in range(parts_ref.shape[0]):
        image = image + parts_ref[k]
    image_ref[...] = image
    curve = jnp.sum(own_ref[...] * image, axis=0, keepdims=True)
    curve_ref[...] = jnp.broadcast_to(
        jnp.sum(curve, axis=1, keepdims=True)[None], curve_ref.shape
    )


def gather_image(parts, own, devices):
    return pl.pallas_call(
        gather_kernel,
        in_specs=[VMEM] * 2,
        out_specs=[VMEM] * 2,
        out_shape=[
            jax.ShapeDtypeStruct(own.shape, jnp.float32),
            jax.ShapeDtypeStruct((devices, 8, 128), jnp.float32),
        ],
    )(parts, own)


def advance_kernel(curve_ref, gamma_ref, sides_ref, moves_ref, out_ref):
    curve = curve_ref[0, 0:1, 0:1]
    for k in range(1, curve_ref.shape[0]):
        curve = curve + curve_ref[k, 0:1, 0:1]
    scale = gamma_ref[0:1, 0:1] / curve
    out_ref[0] = sides_ref[0] + scale * moves_ref[0]
    out_ref[1] = sides_ref[1] - scale * moves_ref[1]


def local(points, pivots, right_values, right_derivs):
    row, col = lax.axis_index("row"), lax.axis_index("col")
    row_count, col_count = lax.axis_size("row"), lax.axis_size("col")
    row_total, features = points.shape
    samples = right_values.shape[1]
    width = features + 1

    side = math.isqrt(row_count)
    by_high = [[high * side + low for high in range(side)] for low in range(side)]
    by_low = [[high * side + low for low in range(side)] for high in range(side)]
    point_blocks = spread(points, "row")
    all_points = point_blocks.reshape(-1, features)
    lanes = jnp.arange(samples * features, dtype=jnp.int32)
    picks = (lanes[None, :] == jnp.arange(features, dtype=jnp.int32)[:, None] * samples + col)
    value_picks = (jnp.arange(samples, dtype=jnp.int32) == col)[None, :]
    residual = jnp.concatenate(
        [wide_dot(picks, right_derivs, (1, 1)), wide_dot(value_picks, right_values, (1, 1))],
        axis=0,
    )

    pivot_data = pivot_table(all_points, turned(pivots, col * SHARE))
    own_turned = jnp.transpose(points.astype(jnp.float32))
    rank = pivots.shape[0]
    lead, extra, sums = make_factor(
        (pivot_data[0], pivot_data[4], pivot_data[2]), points, own_turned, residual
    )
    factor = (pivot_data[0], own_turned, lead, extra, jnp.transpose(pivot_data[2]))
    sums = jnp.sum(spread(jnp.sum(spread(sums, "row", by_high), axis=0), "row", by_low), axis=0)
    inv = inverse(col[None], spread(sums[:72], "col"), pivot_block(pivot_data))

    gamma = jnp.ones((8, 128), jnp.float32)
    direction, copies, gamma = descend(
        factor, inv, sums[None, 72:], residual, jnp.zeros_like(residual), gamma, side
    )
    estimate = jnp.zeros_like(residual)
    for iteration in range(ITERS):
        fields = lax.all_to_all(
            copies, "row", 0, 0, axis_index_groups=by_high, tiled=True
        )
        parts = lax.all_to_all(
            image_part(row[None], fields, point_blocks),
            "row", 0, 0, axis_index_groups=by_low, tiled=True,
        )
        image, curve = gather_image(parts, direction, row_count)
        curve = lax.all_to_all(curve, "row", 0, 0, tiled=True)
        if iteration + 1 < ITERS:
            residual, sums, step = project(factor, image, residual, curve, gamma)
            estimate = step[0, 0] * direction
            sums = lax.all_to_all(sums, "row", 0, 0, tiled=True)
            direction, copies, gamma = descend(
                factor, inv, sums, residual, direction, gamma, side
            )
    fields = pl.pallas_call(
        advance_kernel,
        in_specs=[VMEM] * 4,
        out_specs=VMEM,
        out_shape=jax.ShapeDtypeStruct((2, width, row_total), jnp.float32),
    )(curve, gamma, jnp.stack([estimate, residual]), jnp.stack([direction, image]))
    share_rows = row_total // col_count
    fields = fields.reshape(2, width, col_count, share_rows)
    fields = jnp.transpose(fields, (2, 0, 1, 3)).reshape(col_count, -1)
    fields = lax.all_to_all(fields, "col", 0, 0, tiled=True)
    fields = jnp.transpose(fields.reshape(samples, 2, width, share_rows), (1, 3, 2, 0))
    values = fields[:, :, features]
    derivs = fields[:, :, :features].reshape(2, share_rows, features * samples)
    return (values[0], derivs[0], values[1], derivs[1])


def solution(mesh):
    in_specs = (P("row", None), P(), P("row", None), P("row", None))
    out_specs = (P(("row", "col"), None),) * 4
    return jax.shard_map(local, mesh=mesh, in_specs=in_specs, out_specs=out_specs, check_vma=False)
```

```python
import math

import jax
import jax.numpy as jnp
from jax import lax
from jax.experimental import pallas as pl
from jax.experimental.pallas import tpu as pltpu
from jax.sharding import PartitionSpec as P

ITERS = 2
NOISE = 0.5
HIGHEST = lax.Precision.HIGHEST


def spread(block, axis, groups=None):
    size = len(groups[0]) if groups else lax.axis_size(axis)
    copies = jnp.broadcast_to(block[None], (size,) + block.shape)
    return lax.all_to_all(copies, axis, 0, 0, axis_index_groups=groups, tiled=True)


def wide_dot(former, latter, dims):
    return lax.dot_general(
        former.astype(jnp.float32),
        latter.astype(jnp.float32),
        ((dims[0:1], dims[1:2]), ((), ())),
        precision=HIGHEST,
        preferred_element_type=jnp.float32,
    )


def half_dot(former, latter, dims):
    return lax.dot_general(
        former,
        latter,
        ((dims[0:1], dims[1:2]), ((), ())),
        preferred_element_type=jnp.float32,
    )


def pivot_table(all_points, pivots):
    count, features = all_points.shape
    owner_ids = pivots // (features + 1)
    component = pivots % (features + 1)
    picks = (owner_ids[:, None] == jnp.arange(count, dtype=jnp.int32)[None, :]).astype(jnp.bfloat16)
    pivot_pts = half_dot(picks, all_points, (1, 0)).astype(jnp.bfloat16)
    valued = (component == 0).astype(jnp.float32)
    unit_dirs = (component[:, None] - 1 == jnp.arange(features, dtype=jnp.int32)[None, :]).astype(
        jnp.bfloat16
    )
    chosen = jnp.sum(pivot_pts.astype(jnp.float32) * unit_dirs.astype(jnp.float32), axis=1)
    return (pivot_pts, valued, unit_dirs, chosen, component[:, None] - 1)


def turned(array, start):
    return lax.dynamic_slice_in_dim(jnp.concatenate([array, array]), start, array.shape[0], 0)


def square_norms(points):
    return jnp.sum(jnp.square(points.astype(jnp.float32)), axis=1)


def pivot_block(pivot_data):
    pivot_pts, valued, unit_dirs, chosen, _ = pivot_data
    norms = square_norms(pivot_pts)
    dots = half_dot(pivot_pts, pivot_pts, (1, 1))
    kernel = jnp.exp(-0.5 * (norms[:, None] + norms[None, :] - 2.0 * dots))
    select = half_dot(pivot_pts, unit_dirs, (1, 1))
    after_terms = select - chosen[None, :]
    before = chosen[:, None] - jnp.transpose(select)
    unit_dots = half_dot(unit_dirs, unit_dirs, (1, 1))
    mixed_terms = (
        valued[:, None] * valued[None, :] + valued[:, None] * after_terms - valued[None, :] * before
    )
    return kernel * (mixed_terms + unit_dots - before * after_terms)


def pair_inverse(first, cross, second):
    scale = 1.0 / (first * second - cross * cross)
    return (second * scale, -cross * scale, first * scale)


def inverse_four(a):
    p0, p1, p2 = pair_inverse(a(0, 0), a(1, 0), a(1, 1))
    q00, q01, q10, q11 = a(2, 0), a(3, 0), a(2, 1), a(3, 1)
    t00, t01 = q00 * p0 + q10 * p1, q00 * p1 + q10 * p2
    t10, t11 = q01 * p0 + q11 * p1, q01 * p1 + q11 * p2
    w00 = a(2, 2) - (t00 * q00 + t01 * q10)
    w01 = a(3, 2) - (t10 * q00 + t11 * q10)
    w11 = a(3, 3) - (t10 * q01 + t11 * q11)
    v0, v1, v2 = pair_inverse(w00, w01, w11)
    s00, s01 = v0 * t00 + v1 * t10, v0 * t01 + v1 * t11
    s10, s11 = v1 * t00 + v2 * t10, v1 * t01 + v2 * t11
    i00 = p0 + (t00 * s00 + t10 * s10)
    i01 = p1 + (t00 * s01 + t10 * s11)
    i11 = p2 + (t01 * s01 + t11 * s11)
    return (
        (i00, i01, -s00, -s10),
        (i01, i11, -s01, -s11),
        (-s00, -s01, v0, v1),
        (-s10, -s11, v1, v2),
    )


def dot_four(left, right):
    return (left[0] * right[0] + left[1] * right[1]) + (left[2] * right[2] + left[3] * right[3])


def sweep_eight(mat, top, lane, sub):
    n = mat.shape[0]
    cols = [jnp.broadcast_to(mat[:, top + q : top + q + 1], mat.shape) for q in range(8)]

    def entry(p, q):
        p, q = max(p, q), min(p, q)
        return jnp.broadcast_to(cols[q][top + p : top + p + 1, :], (8, n))

    cross = [[entry(4 + q, k) for q in range(4)] for k in range(4)]
    first = inverse_four(entry)
    turn = [[dot_four(first[k], [cross[l][q] for l in range(4)]) for q in range(4)] for k in range(4)]

    def left_over(p, q):
        return entry(4 + p, 4 + q) - dot_four(
            [cross[k][p] for k in range(4)], [turn[k][q] for k in range(4)]
        )

    second = inverse_four(left_over)
    front = (lane >= top) & (lane < top + 4)
    back = (lane >= top + 4) & (lane < top + 8)
    inside = front | back
    unit = [jnp.where(lane == top + p, 1.0, 0.0) for p in range(8)]
    rows = [jnp.broadcast_to(mat[top + p : top + p + 1, :], (8, n)) for p in range(8)]
    ahead = [jnp.where(front, unit[p], rows[p]) for p in range(4)]
    ahead = [dot_four(first[k], ahead) for k in range(4)]
    after = [
        jnp.where(
            back,
            unit[4 + p],
            jnp.where(front, 0.0, rows[4 + p]) - dot_four([cross[k][p] for k in range(4)], ahead),
        )
        for p in range(4)
    ]
    after = [dot_four(second[p], after) for p in range(4)]
    ahead = [jnp.where(back, 0.0, ahead[k]) - dot_four(turn[k], after) for k in range(4)]
    pivot_rows = ahead + after
    tiles = []
    for s in range(0, n, 8):
        if s == top:
            tile = pivot_rows[0]
            for p in range(1, 8):
                tile = jnp.where(sub == p, pivot_rows[p], tile)
        else:
            here = [cols[p][s : s + 8] for p in range(8)]
            tile = jnp.where(inside, 0.0, mat[s : s + 8]) - (
                dot_four(here[:4], pivot_rows[:4]) + dot_four(here[4:], pivot_rows[4:])
            )
        tiles.append(tile)
    return jnp.concatenate(tiles, axis=0)


SWEEP = 128
VMEM = pl.BlockSpec(memory_space=pltpu.VMEM)
SHARE = 32


def inverse_kernel(turn_ref, bands_ref, kpp_ref, out_ref, diag_ref):
    size = out_ref.shape[0]
    bands = size // SHARE
    lane = lax.broadcasted_iota(jnp.int32, (SHARE, 128), 1)
    for k in range(bands):
        packed = bands_ref[k, 2 * SHARE : 2 * SHARE + 8]
        corner = jnp.concatenate(
            [packed] + [pltpu.roll(packed, 128 - SHARE * u, 1) for u in range(1, 4)], axis=0
        )
        band = jnp.concatenate(
            [
                jnp.where(lane < SHARE, 0.5, 1.0) * bands_ref[k, 0:SHARE],
                bands_ref[k, SHARE : 2 * SHARE],
                jnp.where(lane < SHARE, 0.5 * corner, 0.0),
                jnp.zeros((SHARE, size - 384), jnp.float32),
            ],
            axis=1,
        )
        place = pl.multiple_of(lax.rem(k + bands - turn_ref[0], bands) * SHARE, SHARE)
        out_ref[pl.ds(place, SHARE)] = pltpu.roll(band, place, 1)
    out_ref[...] = out_ref[...] + jnp.transpose(out_ref[...]) + NOISE * kpp_ref[...]
    lane = lax.broadcasted_iota(jnp.int32, (8, SWEEP), 1)
    sub = lax.broadcasted_iota(jnp.int32, (8, SWEEP), 0)

    def dot(former, latter):
        return jnp.dot(former, latter, precision=HIGHEST, preferred_element_type=jnp.float32)

    count = size // SWEEP
    spans = [slice(k * SWEEP, (k + 1) * SWEEP) for k in range(count)]
    diag = out_ref[spans[0], spans[0]]
    for k in range(count):
        for top in range(0, SWEEP, 8):
            diag = sweep_eight(diag, top, lane, sub)
        diag_ref[...] = diag
        here = diag_ref[...]
        row = [here if c == k else dot(here, out_ref[spans[k], spans[c]]) for c in range(count)]
        if k + 1 < count:
            ahead = spans[k + 1]
            diag = out_ref[ahead, ahead] - dot(out_ref[ahead, spans[k]], row[k + 1])
        for r in range(count):
            if r == k:
                continue
            column = out_ref[spans[r], spans[k]]
            for c in range(count):
                if c == k:
                    out_ref[spans[r], spans[c]] = -dot(column, here)
                elif r == c == k + 1:
                    out_ref[spans[r], spans[c]] = diag
                else:
                    out_ref[spans[r], spans[c]] = out_ref[spans[r], spans[c]] - dot(column, row[c])
        for c in range(count):
            out_ref[spans[k], spans[c]] = row[c]


def inverse(turn, bands, kpp):
    vmem = pl.BlockSpec(memory_space=pltpu.VMEM)
    return pl.pallas_call(
        inverse_kernel,
        out_shape=jax.ShapeDtypeStruct(kpp.shape, jnp.float32),
        in_specs=[pl.BlockSpec(memory_space=pltpu.SMEM), vmem, vmem],
        out_specs=vmem,
        scratch_shapes=[pltpu.VMEM((SWEEP, SWEEP), jnp.float32)],
        compiler_params=pltpu.CompilerParams(vmem_limit_bytes=20 * 2**20),
        cost_estimate=pl.CostEstimate(
            flops=10**9, bytes_accessed=3 * 2**20, transcendentals=0
        ),
    )(turn, bands, kpp)


def dot_nt(former, latter):
    return lax.dot_general(
        former, latter, (((1,), (1,)), ((), ())), preferred_element_type=jnp.float32
    )


def thirds_rows(row, count):
    high = row.astype(jnp.bfloat16).astype(jnp.float32)
    middle = (row - high).astype(jnp.bfloat16).astype(jnp.float32)
    low = row - high - middle
    sub = lax.broadcasted_iota(jnp.int32, (count, row.shape[1]), 0)
    parts = jnp.where(
        sub == 0, high, jnp.where(sub == 1, middle, jnp.where(sub == 2, low, jnp.zeros_like(low)))
    )
    return parts.astype(jnp.bfloat16)


def plain_rows(u, columns, lines, lead):
    return (columns[:, u : u + 1] - lines[u : u + 1]) * lead


def each_dimension(pivots_ref, columns_ref, features, start, body):
    columns_ref[:, 0:features] = pivots_ref[...].astype(jnp.float32)

    def group(step, carry):
        columns = columns_ref[...]
        place = pl.ds(pl.multiple_of(step * UNROLL, UNROLL), UNROLL)
        carry = body(step, place, columns, carry)
        columns_ref[...] = pltpu.roll(columns, columns.shape[1] - UNROLL, 1)
        return carry

    return lax.fori_loop(0, features // UNROLL, group, start)


def factor_kernel(
    pivots_ref, dirs_ref, comp_ref, points_ref, turned_ref, field_ref,
    lead_ref, extra_ref, sums_ref, kern_ref, comps_ref, total_ref, columns_ref,
):
    features = turned_ref.shape[0]
    rank = lead_ref.shape[0]

    def add(rows, line):
        left = jnp.concatenate([rows[:SHARE], thirds_rows(line, 16)], axis=0)
        total_ref[...] += dot_nt(left, rows)

    pivot_pts = pivots_ref[...]
    wide_pts = pivot_pts.astype(jnp.float32)
    wide_dirs = dirs_ref[...].astype(jnp.float32)
    norms = jnp.sum(wide_pts * wide_pts, axis=1, keepdims=True)
    chosen = jnp.sum(wide_pts * wide_dirs, axis=1, keepdims=True)
    valued = jnp.where(comp_ref[...] < 0, 1.0, 0.0)
    own_norms = jnp.sum(turned_ref[...] * turned_ref[...], axis=0, keepdims=True)
    dots = dot_nt(pivot_pts, points_ref[...])
    kern = jnp.exp(-0.5 * (own_norms + norms - 2.0 * dots))
    along = dot_nt(dirs_ref[...], points_ref[...]) - chosen
    lead = kern * (valued + along)
    kern_ref[...] = kern
    lead_ref[...] = lead
    plain = -along * lead
    extra = (kern + plain).astype(jnp.bfloat16).astype(jnp.float32) - plain.astype(
        jnp.bfloat16
    ).astype(jnp.float32)
    extra_ref[...] = jnp.where(comp_ref[...] < 0, 0.0, extra)
    comps_ref[...] = jnp.broadcast_to(comp_ref[...], comps_ref.shape)
    total_ref[...] = jnp.zeros_like(total_ref)
    add(lead.astype(jnp.bfloat16), field_ref[features : features + 1])

    def body(step, place, columns, carry):
        lines, field = turned_ref[place], field_ref[place]
        for u in range(UNROLL):
            plain = plain_rows(u, columns, lines, lead_ref[...])
            here = comps_ref[...] == step * UNROLL + u
            rows = jnp.where(here, kern_ref[...] + plain, plain)
            add(rows.astype(jnp.bfloat16), field[u : u + 1])
        return carry

    each_dimension(pivots_ref, columns_ref, features, 0, body)
    sums_ref[0:SHARE] = total_ref[0:SHARE, 0:128]
    sums_ref[SHARE : 2 * SHARE] = total_ref[0:SHARE, 128:256]
    lane = lax.broadcasted_iota(jnp.int32, (8, 128), 1)
    corner = jnp.zeros((8, 128), jnp.float32)
    for u in range(4):
        piece = total_ref[8 * u : 8 * u + 8, 256:384]
        piece = pltpu.roll(piece, SHARE * u, 1) if u else piece
        corner = jnp.where((lane >= SHARE * u) & (lane < SHARE * (u + 1)), piece, corner)
    sums_ref[2 * SHARE : 2 * SHARE + 8] = corner
    high = total_ref[SHARE : SHARE + 1]
    full = high + (total_ref[SHARE + 1 : SHARE + 2] + total_ref[SHARE + 2 : SHARE + 3])
    for u in range(rank // 128):
        sums_ref[72 + u : 73 + u] = high[:, 128 * u : 128 * u + 128]
        sums_ref[76 + u : 77 + u] = full[:, 128 * u : 128 * u + 128]
    field = field_ref[0 : features + 1]
    square = jnp.sum(jnp.sum(field * field, axis=0, keepdims=True), axis=1, keepdims=True)
    sums_ref[80:88] = jnp.broadcast_to(square, (8, 128))


UNROLL = 16


def make_factor(pivot_data, points, turned_points, field):
    pivot_pts, comp, dirs = pivot_data
    rank, features = pivot_pts.shape
    count = points.shape[0]
    return pl.pallas_call(
        factor_kernel,
        in_specs=[VMEM] * 6,
        out_specs=[VMEM] * 3,
        out_shape=[
            jax.ShapeDtypeStruct((rank, count), jnp.float32),
            jax.ShapeDtypeStruct((rank, count), jnp.float32),
            jax.ShapeDtypeStruct((88, 128), jnp.float32),
        ],
        scratch_shapes=[
            pltpu.VMEM((rank, count), jnp.float32),
            pltpu.VMEM((rank, count), jnp.int32),
            pltpu.VMEM((SHARE + 16, rank), jnp.float32),
            pltpu.VMEM((rank, 128), jnp.float32),
        ],
        compiler_params=pltpu.CompilerParams(vmem_limit_bytes=20 * 2**20),
        cost_estimate=pl.CostEstimate(
            flops=2 * 48 * 65 * rank * count, bytes_accessed=4 * 2**20, transcendentals=rank * count
        ),
    )(pivot_pts, dirs, comp, points, turned_points, field)


def descend_kernel(
    pivots_ref, turned_ref, lead_ref, extra_ref, picks_ref, inv_ref, sums_ref, field_ref, old_ref,
    gamma_ref, out_ref, copies_ref, new_gamma_ref, coef_ref, columns_ref,
):
    features = field_ref.shape[0] - 1
    lines = sums_ref[0]
    for k in range(1, sums_ref.shape[0]):
        lines = lines + sums_ref[k]
    low = jnp.concatenate([lines[u : u + 1] for u in range(4)], axis=1)
    full = jnp.concatenate([lines[u : u + 1] for u in range(4, 8)], axis=1)
    coef = jnp.dot(
        jnp.broadcast_to(low, (8, low.shape[1])),
        inv_ref[...],
        precision=HIGHEST,
        preferred_element_type=jnp.float32,
    )[0:1]
    coef_ref[...] = thirds_rows(coef, 16)
    gamma = (lines[8:9, 0:1] - jnp.sum(full * coef, axis=1, keepdims=True)) / NOISE
    new_gamma_ref[...] = jnp.broadcast_to(gamma, (8, 128))
    beta = gamma / gamma_ref[0:1, 0:1]

    def apply(rows):
        parts = jnp.dot(
            coef_ref[...], rows.astype(jnp.bfloat16), preferred_element_type=jnp.float32
        )
        return parts[0:1] + (parts[1:2] + parts[2:3])

    out_ref[features : features + 1] = apply(lead_ref[...])
    out_ref[0:features] = jnp.dot(
        picks_ref[...].astype(jnp.float32) * coef,
        extra_ref[...],
        precision=HIGHEST,
        preferred_element_type=jnp.float32,
    )

    def body(step, place, columns, carry):
        lines = turned_ref[place]
        rows = [apply(plain_rows(u, columns, lines, lead_ref[...])) for u in range(UNROLL)]
        out_ref[place] += jnp.concatenate(rows, axis=0)
        return carry

    each_dimension(pivots_ref, columns_ref, features, 0, body)
    out_ref[...] = (field_ref[...] - out_ref[...]) / NOISE + beta * old_ref[...]
    copies_ref[...] = jnp.broadcast_to(out_ref[...][None], copies_ref.shape)


def descend(factor, inv, sums, field, old, gamma, copies):
    rank, count = factor[2].shape
    return pl.pallas_call(
        descend_kernel,
        in_specs=[VMEM] * 10,
        out_specs=[VMEM] * 3,
        out_shape=[
            jax.ShapeDtypeStruct(field.shape, jnp.float32),
            jax.ShapeDtypeStruct((copies,) + field.shape, jnp.float32),
            jax.ShapeDtypeStruct((8, 128), jnp.float32),
        ],
        scratch_shapes=[pltpu.VMEM((16, rank), jnp.bfloat16), pltpu.VMEM((rank, 128), jnp.float32)],
        compiler_params=pltpu.CompilerParams(vmem_limit_bytes=20 * 2**20),
        cost_estimate=pl.CostEstimate(
            flops=2 * 16 * 65 * rank * count, bytes_accessed=5 * 2**20, transcendentals=0
        ),
    )(*factor, inv, sums, field, old, gamma)


def project_kernel(
    pivots_ref, turned_ref, lead_ref, extra_ref, picks_ref, image_ref, field_ref, curve_ref,
    gamma_ref, next_ref, sums_ref, step_ref, columns_ref,
):
    features = field_ref.shape[0] - 1
    curve = curve_ref[0, 0:1, 0:1]
    for k in range(1, curve_ref.shape[0]):
        curve = curve + curve_ref[k, 0:1, 0:1]
    scale = gamma_ref[0:1, 0:1] / curve
    step_ref[...] = jnp.broadcast_to(scale, (8, 128))
    next_ref[...] = field_ref[...] - scale * image_ref[...]

    def add(line, rows):
        return dot_nt(thirds_rows(line, 16), rows.astype(jnp.bfloat16))

    total = add(next_ref[features : features + 1], lead_ref[...])

    def body(step, place, columns, total):
        lines, field = turned_ref[place], next_ref[place]
        for u in range(UNROLL):
            rows = plain_rows(u, columns, lines, lead_ref[...])
            total = total + add(field[u : u + 1], rows)
        return total

    total = each_dimension(pivots_ref, columns_ref, features, total, body)
    field = next_ref[...]
    upper = field[0:features].astype(jnp.bfloat16)
    rest = field[0:features] - upper.astype(jnp.float32)
    middle = rest.astype(jnp.bfloat16)
    lower = (rest - middle.astype(jnp.float32)).astype(jnp.bfloat16)

    def meet(part):
        return lax.dot_general(
            picks_ref[...], part, (((0,), (0,)), ((), ())), preferred_element_type=jnp.float32
        )

    first = meet(upper)
    ones = jnp.ones((8, field.shape[1]), jnp.float32)
    both = [
        lax.dot_general(
            ones,
            extra_ref[...] * part,
            (((1,), (1,)), ((), ())),
            precision=HIGHEST,
            preferred_element_type=jnp.float32,
        )[0:1]
        for part in (first, first + (meet(middle) + meet(lower)))
    ]
    high = total[0:1] + both[0]
    full = total[0:1] + (total[1:2] + total[2:3]) + both[1]
    lines = [line[:, 128 * u : 128 * u + 128] for line in (high, full) for u in range(4)]
    square = jnp.sum(jnp.sum(field * field, axis=0, keepdims=True), axis=1, keepdims=True)
    lines = jnp.concatenate(lines + [jnp.broadcast_to(square, (8, 128))], axis=0)
    sums_ref[...] = jnp.broadcast_to(lines[None], sums_ref.shape)


def project(factor, image, field, curve, gamma):
    rank, count = factor[2].shape
    return pl.pallas_call(
        project_kernel,
        in_specs=[VMEM] * 9,
        out_specs=[VMEM] * 3,
        out_shape=[
            jax.ShapeDtypeStruct(field.shape, jnp.float32),
            jax.ShapeDtypeStruct((curve.shape[0], 16, 128), jnp.float32),
            jax.ShapeDtypeStruct((8, 128), jnp.float32),
        ],
        scratch_shapes=[pltpu.VMEM((rank, 128), jnp.float32)],
        compiler_params=pltpu.CompilerParams(vmem_limit_bytes=20 * 2**20),
        cost_estimate=pl.CostEstimate(
            flops=2 * 16 * 65 * rank * count, bytes_accessed=4 * 2**20, transcendentals=0
        ),
    )(*factor, image, field, curve, gamma)


def image_kernel(place_ref, fields_ref, points_ref, image_ref):
    blocks, width, count = fields_ref.shape
    features = width - 1
    high_place, low_place = place_ref[0] // blocks, lax.rem(place_ref[0], blocks)

    def dot(former, latter):
        return jnp.dot(former, latter, preferred_element_type=jnp.float32)

    sides = []
    for k in range(blocks):
        points = points_ref[k * blocks + low_place]
        spare = jnp.zeros((count, features), jnp.float32)
        wide = jnp.concatenate([points.astype(jnp.float32), spare], axis=1)
        turned_points = jnp.transpose(wide)[0:features]
        lane = lax.broadcasted_iota(jnp.int32, wide.shape, 1)
        with_ones = jnp.where(lane == features, 1.0, wide).astype(jnp.bfloat16)
        slopes = fields_ref[k, 0:features]
        owned = fields_ref[k, features : features + 1] - jnp.sum(
            turned_points * slopes, axis=0, keepdims=True
        )
        norms = jnp.sum(turned_points * turned_points, axis=0, keepdims=True)
        high = slopes.astype(jnp.bfloat16)
        rest = slopes - high.astype(jnp.float32)
        middle = rest.astype(jnp.bfloat16)
        low = (rest - middle.astype(jnp.float32)).astype(jnp.bfloat16)
        sides.append((with_ones, owned, norms, high, middle, low))

    def rows(j, carry):
        points = points_ref[high_place * blocks + j]
        wide = points.astype(jnp.float32)
        own_norms = jnp.sum(wide * wide, axis=1, keepdims=True)
        thrice = jnp.concatenate([points] * 3, axis=1)
        total = jnp.zeros((count, 2 * features), jnp.float32)
        base = jnp.zeros((count, 2 * features), jnp.float32)
        for k in range(blocks):
            with_ones, owned, norms, high, middle, low = sides[k]
            dots = dot_nt(points, points_ref[k * blocks + low_place])
            kern = jnp.exp(-0.5 * (own_norms + norms - 2.0 * dots))
            cross = dot(thrice, jnp.concatenate([high, middle, low], axis=0))
            weight = kern * (cross + owned)
            upper = weight.astype(jnp.bfloat16)
            lower = (weight - upper.astype(jnp.float32)).astype(jnp.bfloat16)
            total += dot(upper, with_ones) + dot(lower, with_ones)
            upper = kern.astype(jnp.bfloat16)
            lower = (kern - upper.astype(jnp.float32)).astype(jnp.bfloat16)
            base += dot_nt(upper, jnp.concatenate([high, middle], axis=0)) + dot_nt(
                lower, jnp.concatenate([high, jnp.zeros_like(high)], axis=0)
            )
        value = total[:, features : features + 1]
        spare = jnp.zeros((count, features), jnp.float32)
        total += jnp.concatenate(
            [base[:, 0:features] + base[:, features:] - wide * value, spare], axis=1
        )
        image_ref[j] = jnp.transpose(total)[0:width]
        return carry

    for j in range(blocks):
        rows(j, 0)


def image_part(place, fields, points):
    blocks, width, count = fields.shape
    return pl.pallas_call(
        image_kernel,
        in_specs=[pl.BlockSpec(memory_space=pltpu.SMEM), VMEM, VMEM],
        out_specs=VMEM,
        out_shape=jax.ShapeDtypeStruct((blocks, width, count), jnp.float32),
        compiler_params=pltpu.CompilerParams(vmem_limit_bytes=24 * 2**20),
        cost_estimate=pl.CostEstimate(
            flops=2 * 5 * blocks * blocks * count * count * 128,
            bytes_accessed=2**20,
            transcendentals=blocks * blocks * count * count,
        ),
    )(place, fields, points)


def gather_kernel(parts_ref, own_ref, image_ref, curve_ref):
    image = NOISE * own_ref[...]
    for k in range(parts_ref.shape[0]):
        image = image + parts_ref[k]
    image_ref[...] = image
    curve = jnp.sum(own_ref[...] * image, axis=0, keepdims=True)
    curve_ref[...] = jnp.broadcast_to(
        jnp.sum(curve, axis=1, keepdims=True)[None], curve_ref.shape
    )


def gather_image(parts, own, devices):
    return pl.pallas_call(
        gather_kernel,
        in_specs=[VMEM] * 2,
        out_specs=[VMEM] * 2,
        out_shape=[
            jax.ShapeDtypeStruct(own.shape, jnp.float32),
            jax.ShapeDtypeStruct((devices, 8, 128), jnp.float32),
        ],
    )(parts, own)


def advance_kernel(curve_ref, gamma_ref, sides_ref, moves_ref, out_ref):
    curve = curve_ref[0, 0:1, 0:1]
    for k in range(1, curve_ref.shape[0]):
        curve = curve + curve_ref[k, 0:1, 0:1]
    scale = gamma_ref[0:1, 0:1] / curve
    out_ref[0] = sides_ref[0] + scale * moves_ref[0]
    out_ref[1] = sides_ref[1] - scale * moves_ref[1]


def local(points, pivots, right_values, right_derivs):
    row, col = lax.axis_index("row"), lax.axis_index("col")
    row_count, col_count = lax.axis_size("row"), lax.axis_size("col")
    row_total, features = points.shape
    samples = right_values.shape[1]
    width = features + 1

    side = math.isqrt(row_count)
    by_high = [[high * side + low for high in range(side)] for low in range(side)]
    by_low = [[high * side + low for low in range(side)] for high in range(side)]
    point_blocks = spread(points, "row")
    all_points = point_blocks.reshape(-1, features)
    lanes = jnp.arange(samples * features, dtype=jnp.int32)
    picks = (lanes[None, :] == jnp.arange(features, dtype=jnp.int32)[:, None] * samples + col)
    value_picks = (jnp.arange(samples, dtype=jnp.int32) == col)[None, :]
    residual = jnp.concatenate(
        [wide_dot(picks, right_derivs, (1, 1)), wide_dot(value_picks, right_values, (1, 1))],
        axis=0,
    )

    pivot_data = pivot_table(all_points, turned(pivots, col * SHARE))
    own_turned = jnp.transpose(points.astype(jnp.float32))
    rank = pivots.shape[0]
    lead, extra, sums = make_factor(
        (pivot_data[0], pivot_data[4], pivot_data[2]), points, own_turned, residual
    )
    factor = (pivot_data[0], own_turned, lead, extra, jnp.transpose(pivot_data[2]))
    sums = jnp.sum(spread(jnp.sum(spread(sums, "row", by_high), axis=0), "row", by_low), axis=0)
    inv = inverse(col[None], spread(sums[:72], "col"), pivot_block(pivot_data))

    gamma = jnp.ones((8, 128), jnp.float32)
    direction, copies, gamma = descend(
        factor, inv, sums[None, 72:], residual, jnp.zeros_like(residual), gamma, side
    )
    estimate = jnp.zeros_like(residual)
    for iteration in range(ITERS):
        fields = lax.all_to_all(
            copies, "row", 0, 0, axis_index_groups=by_high, tiled=True
        )
        parts = lax.all_to_all(
            image_part(row[None], fields, point_blocks),
            "row", 0, 0, axis_index_groups=by_low, tiled=True,
        )
        image, curve = gather_image(parts, direction, row_count)
        curve = lax.all_to_all(curve, "row", 0, 0, tiled=True)
        if iteration + 1 < ITERS:
            residual, sums, step = project(factor, image, residual, curve, gamma)
            estimate = step[0, 0] * direction
            sums = lax.all_to_all(sums, "row", 0, 0, tiled=True)
            direction, copies, gamma = descend(
                factor, inv, sums, residual, direction, gamma, side
            )
    fields = pl.pallas_call(
        advance_kernel,
        in_specs=[VMEM] * 4,
        out_specs=VMEM,
        out_shape=jax.ShapeDtypeStruct((2, width, row_total), jnp.float32),
    )(curve, gamma, jnp.stack([estimate, residual]), jnp.stack([direction, image]))
    share_rows = row_total // col_count
    fields = fields.reshape(2, width, col_count, share_rows)
    fields = jnp.transpose(fields, (2, 0, 1, 3)).reshape(col_count, -1)
    fields = lax.all_to_all(fields, "col", 0, 0, tiled=True)
    fields = jnp.transpose(fields.reshape(samples, 2, width, share_rows), (1, 3, 2, 0))
    values = fields[:, :, features]
    derivs = fields[:, :, :features].reshape(2, share_rows, features * samples)
    return (values[0], derivs[0], values[1], derivs[1])


def solution(mesh):
    in_specs = (P("row", None), P(), P("row", None), P("row", None))
    out_specs = (P(("row", "col"), None),) * 4
    return jax.shard_map(local, mesh=mesh, in_specs=in_specs, out_specs=out_specs, check_vma=False)
```
